128 devices in a mesh: gx: 4 (over x), gy: 16 (over z, y), gz: 2 (over core).
Axes of the slice: x: 4, y: 4, z: 4, core: 2. Of those that a mesh axis runs over, the one named last changes fastest.
Arguments:
- tensor: float32 [128, 1024, 128, 32], P('gx', 'gy', 'gz'), may hold values from -6 to 6
- factor_one: float32 [128, 64], P('gx'), may hold values from -0.5 to 0.5
- factor_two: float32 [1024, 64], P('gy'), may hold values from -0.1875 to 0.1875
- factor_three: float32 [128, 64], P('gz'), may hold values from -0.5 to 0.5
- species_factor: float32 [32, 16], replicated, may hold values from -1 to 1
Outputs:
- new_one: float32 [128, 64], P('gx')
- new_two: float32 [1024, 64], P('gy')
The draws below stay inside these ranges and needn't reach their ends.
All inputs are finite; a program needn't handle non-finite values.
Results may differ from the reference program's by a relative error of at most 0.0003.
Values sent between devices are 32-bit elements; how exact they have to be, the bound alone decides.
No kernel may reach another device: no remote copies, remote signals or barrier semaphores. Data moves between devices by JAX's collectives and lax.ppermute only.
A program may use at most 192 MiB of HBM per device.

```python
import math
import jax
import jax.numpy as jnp
from jax import lax

S = 32
R1 = 64
R2 = 64
R3 = 64
R4 = 16
I1 = 128
I2 = 1024
I3 = 128


def levels(own_key, shape, shards, low, top_value):
    level = 1.0
    for axis_at, shards_of in shards:
        heights = jax.random.uniform(jax.random.fold_in(jax.random.fold_in(own_key, 6), axis_at), (shards_of,), jnp.float32, low / len(shards), top_value / len(shards))
        level = level * jnp.repeat(jnp.exp(heights), shape[axis_at] // shards_of).reshape((-1,) + (1,) * (len(shape) - 1 - axis_at))
    return level


def noise(own_key, shape, deviation, reach, cuts=(), dtype=jnp.bfloat16):
    array = deviation * jax.random.normal(own_key, shape, jnp.float32)
    if cuts:
        array = array * levels(own_key, shape, cuts, -0.22, 0.18)
    return jnp.clip(array, -reach, reach).astype(dtype)


def setup_inputs(seed: int = 0) -> dict:
    seeds = jax.random.split(jax.random.key(seed), 6)
    return {
        "tensor": noise(seeds[0], (I1, I2, I3, S), 1.0, 6.0, ((0, 4), (1, 16), (2, 2)), jnp.float32),
        "factor_one": noise(seeds[1], (I1, R1), I1 ** -0.5, 0.5, ((0, 4),), jnp.float32),
        "factor_two": noise(seeds[2], (I2, R2), I2 ** -0.5, 0.1875, ((0, 16),), jnp.float32),
        "factor_three": noise(seeds[3], (I3, R3), I3 ** -0.5, 0.5, ((0, 2),), jnp.float32),
        "species_factor": noise(seeds[4], (S, R4), S ** -0.5, 1.0, (), jnp.float32),
    }


def orthonormal(image):
    normal_matrix = jnp.dot(image.T, image, precision=lax.Precision.HIGHEST)
    lower = jnp.linalg.cholesky(normal_matrix)
    return jax.scipy.linalg.solve_triangular(lower, image.T, lower=True).T

def reference(tensor, factor_one, factor_two, factor_three, species_factor):
    high = lax.Precision.HIGHEST
    species_cut = jnp.einsum('abcs,sq->abcq', tensor, species_factor, precision=high)
    core_cut = jnp.einsum('abcq,cr->abrq', species_cut, factor_three, precision=high)
    first_unf = jnp.einsum('abrq,bp->aprq', core_cut, factor_two, precision=high).reshape(I1, -1)
    first_gram = jnp.dot(first_unf, first_unf.T, precision=high)
    basis_one = orthonormal(jnp.dot(first_gram, factor_one, precision=high))
    second_unf = jnp.einsum('abrq,ap->bprq', core_cut, basis_one, precision=high).reshape(I2, -1)
    second_gram = jnp.dot(second_unf, second_unf.T, precision=high)
    basis_two = orthonormal(jnp.dot(second_gram, factor_two, precision=high))
    return (basis_one * math.sqrt(I1), basis_two * math.sqrt(I2))
```

```python
import functools
import math

import jax
import jax.numpy as jnp
from jax import lax
from jax.experimental import pallas as pl
from jax.experimental.pallas import tpu as pltpu
from jax.sharding import PartitionSpec as P

F32, BF16 = jnp.float32, jnp.bfloat16
NN = (((1,), (0,)), ((), ()))
NT = (((1,), (1,)), ((), ()))
TN = (((0,), (0,)), ((), ()))
ALL = ("gx", "gy", "gz")
PAIRS = 8
VMEM = pl.BlockSpec(memory_space=pltpu.VMEM)
PARAMS = pltpu.CompilerParams(vmem_limit_bytes=48 << 20)


def split(x):
    hi = x.astype(BF16)
    return hi, (x - hi.astype(F32)).astype(BF16)


def mm(a, b, dims):
    return lax.dot_general(a, b, dims, preferred_element_type=F32)


def mm3(a, b, dims):
    return mm(a[0], b[0], dims) + (mm(a[0], b[1], dims) + mm(a[1], b[0], dims))


def mm_f32(a, b, dims):
    return mm3(split(a), split(b), dims)


def wide(w):
    zero = jnp.zeros_like(w[0])
    return jnp.concatenate([jnp.concatenate(w, 1), jnp.concatenate([w[0], zero], 1)], 0)


def mm_wide(x, w):
    y = mm(jnp.concatenate(split(x), 1), w, NN)
    return y[:, :128] + y[:, 128:]


def iota(shape, dim):
    return lax.broadcasted_iota(jnp.int32, shape, dim)


def ones_where(mask):
    return jnp.where(mask, 1.0, 0.0).astype(BF16)


def spread(left, x, right, mask):
    return tuple(
        jnp.where(mask, mm(mm(left, part, NN).astype(BF16), right, NN), 0.0).astype(BF16)
        for part in split(x)
    )


def core_kernel(first, gz_ref, t_hbm, sft_ref, f3_ref, own_ref, peer_ref, t_vmem, xs_ref, sems):
    def copy(i):
        return pltpu.make_async_copy(t_hbm.at[pl.ds(2 * (first + i), 2)], t_vmem.at[i], sems.at[i])

    for i in range(PAIRS):
        copy(i).start()

    q = (iota((128, 16), 0) // 8 + 8 * gz_ref[0]) % 16
    rows = ones_where(q == iota((128, 16), 1))
    columns = ones_where(iota((32, 256), 0) == iota((32, 256), 1) % 32)
    same = iota((128, 256), 0) % 8 == iota((128, 256), 1) // 32
    sf = spread(rows, sft_ref[...], columns, same)
    rows = ones_where(iota((128, 64), 0) % 64 == iota((128, 64), 1))
    r = iota((64, 128), 1) // 8 * 4 + iota((64, 128), 1) % 4
    columns = ones_where(iota((64, 128), 0) == r)
    same = iota((128, 128), 0) // 64 == iota((128, 128), 1) // 4 % 2
    w3 = wide(spread(rows, f3_ref[...], columns, same))

    def pair(i, _):
        copy(i).wait()
        for g in range(8):
            at = slice(g * 8, g * 8 + 8)
            t = [t_vmem[i, a, at].reshape(256, 64) for a in range(2)]
            th, tl = split(jnp.concatenate(t, 1))
            y = mm(sf[0], jnp.concatenate([th, tl], 1), NN)
            x = y[:, :128] + y[:, 128:] + mm(sf[1], th, NN)
            xs_ref[:, at, :] = x.reshape(16, 8, 128)
        for k in range(8):
            o = mm_wide(xs_ref[2 * k : 2 * k + 2].reshape(128, 128), w3)
            o = o.T.reshape(16, 8, 128)
            if k < 4:
                own_ref[:, k, i] = o
            else:
                peer_ref[:, k - 4, i] = o
        return 0

    lax.fori_loop(0, PAIRS, pair, 0)


def core_cut(first, gz, tensor, sft, f3):
    part = jax.ShapeDtypeStruct((16, 4, PAIRS, 8, 128), F32)
    return pl.pallas_call(
        functools.partial(core_kernel, first),
        in_specs=[pl.BlockSpec(memory_space=pltpu.SMEM), pl.BlockSpec(memory_space=pl.ANY), VMEM, VMEM],
        out_specs=[VMEM, VMEM],
        out_shape=[part, part],
        scratch_shapes=[
            pltpu.VMEM((PAIRS, 2, 64, 32, 64), F32),
            pltpu.VMEM((16, 64, 128), F32),
            pltpu.SemaphoreType.DMA((PAIRS,)),
        ],
        compiler_params=PARAMS,
    )(gz, tensor, sft, f3)


def first_kernel(c_ref, e_ref, gram_ref, fp_ref, g_ref):
    step = pl.program_id(0)

    @pl.when(step == 0)
    def _():
        fp_ref[...] = jnp.zeros_like(fp_ref)

    low = iota((8, 128), 1) < 64
    total = fp_ref[...]
    for y in range(4):
        top, bottom = [], []
        for x in range(4):
            f2 = c_ref[x, y, 128:]
            turned = pltpu.roll(f2, 64, 1)
            top += [jnp.where(low, f2, 0.0), jnp.where(low, turned, 0.0)]
            bottom += [jnp.where(low, 0.0, turned), jnp.where(low, 0.0, f2)]
        w = wide(split(jnp.concatenate(top + bottom, 0)))
        total += mm_wide(c_ref[:, y, :128].reshape(512, 128), w)
    fp_ref[...] = total

    @pl.when(step == pl.num_programs(0) - 1)
    def _():
        gram, cross = jnp.zeros((128, 128), F32), jnp.zeros((128, 128), F32)
        for r in range(4):
            e = fp_ref[pl.ds(r, 128, stride=4), :]
            e_ref[:, r * 128 : (r + 1) * 128] = e
            eh, el = split(e)
            gram += mm(eh, eh, NT)
            cross += mm(eh, el, NT)
        g_ref[...] = gram + (cross + cross.T)
        group = iota((32, 128), 1) // 32
        rows = [g_ref[pl.ds(i, 32, stride=4), :] for i in range(4)]
        for x in range(4):
            block = jnp.zeros((32, 128), F32)
            for i in range(4):
                moved = pltpu.roll(rows[i], 32 * ((i - x) % 4), 1) if i != x else rows[i]
                block = jnp.where(group == i, moved, block)
            gram_ref[x] = block


def first_gram(c):
    return pl.pallas_call(
        first_kernel,
        grid=(4,),
        in_specs=[
            pl.BlockSpec((4, 4, 136, 128), lambda i: (0, i, 0, 0)),
        ],
        out_specs=[
            pl.BlockSpec((128, 512), lambda i: (0, 0)),
            pl.BlockSpec((4, 32, 128), lambda i: (0, 0, 0)),
        ],
        out_shape=[jax.ShapeDtypeStruct((128, 512), F32), jax.ShapeDtypeStruct((4, 32, 128), F32)],
        scratch_shapes=[pltpu.VMEM((512, 128), F32), pltpu.VMEM((128, 128), F32)],
        compiler_params=PARAMS,
    )(c)


def rows_kernel(parts_ref, f1_ref, out_ref):
    row = jnp.sum(parts_ref[...], axis=0, keepdims=True)
    block = jnp.concatenate([row[:, i * 32 : (i + 1) * 32] for i in range(4)] * 2, 0)
    image = mm_f32(block, f1_ref[...], NN)
    image = jnp.concatenate([image[i : i + 1] for i in range(4)], 1)
    out_ref[...] = jnp.broadcast_to(image[None], out_ref.shape)


def image_rows(parts, f1):
    return pl.pallas_call(
        rows_kernel,
        in_specs=[VMEM, VMEM],
        out_specs=VMEM,
        out_shape=jax.ShapeDtypeStruct((128, 1, 256), F32),
        compiler_params=PARAMS,
    )(parts, f1)


def sum_kernel(parts_ref, out_ref):
    out_ref[...] = jnp.broadcast_to(jnp.sum(parts_ref[...], axis=0, keepdims=True), out_ref.shape)


def sum_for_all(parts):
    return pl.pallas_call(
        sum_kernel,
        in_specs=[VMEM],
        out_specs=VMEM,
        out_shape=jax.ShapeDtypeStruct(parts.shape, F32),
        compiler_params=PARAMS,
    )(parts)


def inverse_factor(normal):
    rows, lanes = iota((64, 128), 0), iota((64, 128), 1)
    m = jnp.concatenate([normal, jnp.where(rows == lanes, 1.0, 0.0)[:, :64].astype(F32)], 1)
    for j in range(63):
        row = m[j : j + 1, :]
        column = jnp.where(rows > j, jnp.broadcast_to(m[:, j : j + 1], (64, 128)), 0.0)
        pivot = jnp.broadcast_to(m[j : j + 1, j : j + 1], (1, 128))
        m = m - column * (row / pivot)
    diagonal = jnp.sum(jnp.where(rows == lanes, m, 0.0), axis=1, keepdims=True)
    return m[:, 64:] * lax.rsqrt(diagonal)


def second_kernel(parts_ref, e_ref, c_ref, new_ref, part_ref, i_ref, y_ref, c_vmem, sem):
    copy = pltpu.make_async_copy(c_ref.at[:, :, pl.ds(0, 128)], c_vmem, sem)
    copy.start()
    rows = jnp.sum(parts_ref[...].reshape(4, 32, 256), axis=0)
    for i in range(4):
        i_ref[pl.ds(i, 32, stride=4), :] = rows[:, i * 64 : (i + 1) * 64]
    image = i_ref[...]
    normal = mm_f32(image, image, TN)
    basis = mm_f32(image, inverse_factor(normal), NT)
    new_ref[...] = basis * math.sqrt(128)
    y = mm_f32(mm_f32(basis, basis, NT), e_ref[...], NN)
    for r in range(4):
        y_ref[pl.ds(r, 128, stride=4), :] = y[:, r * 128 : (r + 1) * 128]
    yt = split(y_ref[...].T)
    low = iota((64, 128), 1) < 64
    copy.wait()

    def both(i, _):
        halves = []
        for k in range(2):
            c = split(c_vmem[:, 2 * i + k].reshape(512, 128))
            o = mm3(yt, c, NN)
            halves.append(o[:64, :] + pltpu.roll(o[64:, :], 64, 1))
        part_ref[i] = jnp.where(low, halves[0], pltpu.roll(halves[1], 64, 1))
        return 0

    lax.fori_loop(0, 8, both, 0)


def second_image(parts, e, c):
    return pl.pallas_call(
        second_kernel,
        in_specs=[VMEM, VMEM, pl.BlockSpec(memory_space=pl.ANY)],
        out_specs=[VMEM, VMEM],
        out_shape=[jax.ShapeDtypeStruct((128, 64), F32), jax.ShapeDtypeStruct((8, 64, 128), F32)],
        scratch_shapes=[
            pltpu.VMEM((128, 64), F32),
            pltpu.VMEM((512, 128), F32),
            pltpu.VMEM((4, 16, 128, 128), F32),
            pltpu.SemaphoreType.DMA,
        ],
        compiler_params=PARAMS,
    )(parts, e, c)


def last_kernel(at_ref, image_ref, new_ref):
    normal, cross = jnp.zeros((64, 64), F32), jnp.zeros((64, 64), F32)
    for i in range(8):
        h, l = split(image_ref[i])
        normal += mm(h, h, NT)
        cross += mm(h, l, NT)
    inverse = inverse_factor(normal + (cross + cross.T))
    pair = image_ref[at_ref[0]]
    mine = jnp.where(at_ref[1] == 0, pair[:, :64], pair[:, 64:])
    new_ref[...] = mm_f32(mine, inverse, (((0,), (1,)), ((), ()))) * math.sqrt(1024)


def last_factor(at, image):
    return pl.pallas_call(
        last_kernel,
        in_specs=[pl.BlockSpec(memory_space=pltpu.SMEM), VMEM],
        out_specs=VMEM,
        out_shape=jax.ShapeDtypeStruct((64, 64), F32),
        compiler_params=PARAMS,
    )(at, image)


def to_all(x, names=ALL):
    return lax.all_to_all(x, names, 0, 0, tiled=True)


def swap(x):
    return lax.ppermute(x, "gz", [(0, 1), (1, 0)])


def per_device(tensor, factor_one, factor_two, factor_three, species_factor):
    gx, gy, gz = (lax.axis_index(name).astype(jnp.int32) for name in ALL)

    t = tensor.transpose(0, 1, 3, 2)
    parts = [core_cut(i * PAIRS, gz[None], t, species_factor.T, factor_three) for i in range(2)]
    core = jnp.concatenate([own + swap(peer) for own, peer in parts], axis=2)
    f2 = lax.dynamic_slice_in_dim(factor_two, gx * 16, 16)
    f2 = jnp.broadcast_to(jnp.concatenate([f2[:8], f2[8:]], 1)[None], (64, 8, 128))
    sent = jnp.concatenate([core.reshape(64, 128, 128), f2], 1)
    c = to_all(sent, ("gx", "gy")).reshape(4, 16, 136, 128)

    e, gram = first_gram(c)
    rows = image_rows(to_all(gram.reshape(128, 1, 128)).reshape(128, 128), factor_one)
    new_one, second_part = second_image(to_all(rows).reshape(128, 256), e, c)
    second = to_all(sum_for_all(to_all(second_part.reshape(128, 4, 128)))).reshape(8, 64, 128)
    new_two = last_factor(jnp.stack([gy // 2, gy % 2]), second)
    return lax.dynamic_slice_in_dim(new_one, gx * 32, 32), new_two


def solution(mesh):
    in_specs = (P("gx", "gy", "gz", None), P("gx", None), P("gy", None), P("gz", None), P())
    out_specs = (P("gx", None), P("gy", None))
    return jax.shard_map(
        per_device, mesh=mesh, in_specs=in_specs, out_specs=out_specs, check_vma=False
    )
```

```python
import functools
import math

import jax
import jax.numpy as jnp
from jax import lax
from jax.experimental import pallas as pl
from jax.experimental.pallas import tpu as pltpu
from jax.sharding import PartitionSpec as P

F32, BF16 = jnp.float32, jnp.bfloat16
NN = (((1,), (0,)), ((), ()))
NT = (((1,), (1,)), ((), ()))
TN = (((0,), (0,)), ((), ()))
ALL = ("gx", "gy", "gz")
PAIRS = (12, 4)
SLOTS = 6
VMEM = pl.BlockSpec(memory_space=pltpu.VMEM)
PARAMS = pltpu.CompilerParams(vmem_limit_bytes=12 << 20)
LARGE = pltpu.CompilerParams(vmem_limit_bytes=24 << 20)
HBM = pl.BlockSpec(memory_space=pltpu.HBM)
SMEM = pl.BlockSpec(memory_space=pltpu.SMEM)


def split(x):
    hi = x.astype(BF16)
    return hi, (x - hi.astype(F32)).astype(BF16)


def mm(a, b, dims):
    return lax.dot_general(a, b, dims, preferred_element_type=F32)


def mm3(a, b, dims):
    return mm(a[0], b[0], dims) + (mm(a[0], b[1], dims) + mm(a[1], b[0], dims))


def mm_f32(a, b, dims):
    return mm3(split(a), split(b), dims)


def wide(w):
    zero = jnp.zeros_like(w[0])
    return jnp.concatenate([jnp.concatenate(w, 1), jnp.concatenate([w[0], zero], 1)], 0)


def mm_wide(x, w):
    y = mm(jnp.concatenate(split(x), 1), w, NN)
    return y[:, :128] + y[:, 128:]


def iota(shape, dim):
    return lax.broadcasted_iota(jnp.int32, shape, dim)


def ones_where(mask):
    return jnp.where(mask, 1.0, 0.0).astype(BF16)


def spread(left, x, right, mask):
    return tuple(
        jnp.where(mask, mm(mm(left, part, NN).astype(BF16), right, NN), 0.0).astype(BF16)
        for part in split(x)
    )


def core_kernel(
    first, pairs, gz_ref, t_hbm, factors_ref, own_hbm, peer_hbm, own_ref, peer_ref, t_vmem, xa_ref, xb_ref, sems, out_sems
):
    def copy(i):
        slot = i % SLOTS
        return pltpu.make_async_copy(t_hbm.at[pl.ds(2 * (first + i), 2)], t_vmem.at[slot], sems.at[slot])

    def copies_out(i):
        return [
            pltpu.make_async_copy(ref.at[:, :, pl.ds(i, 2)], hbm.at[:, :, pl.ds(i, 2)], out_sems.at[k, i // 2])
            for k, (ref, hbm) in enumerate(((own_ref, own_hbm), (peer_ref, peer_hbm)))
        ]

    for i in range(min(SLOTS, pairs)):
        copy(i).start()

    q = ((iota((128, 16), 0) >> 3) + 8 * gz_ref[0]) & 15
    rows = ones_where(q == iota((128, 16), 1))
    columns = ones_where(iota((32, 256), 0) == (iota((32, 256), 1) & 31))
    same = (iota((128, 256), 0) & 7) == (iota((128, 256), 1) >> 5)
    sf = spread(rows, factors_ref[:16, 64:96], columns, same)
    rows = ones_where((iota((128, 64), 0) & 63) == iota((128, 64), 1))
    r = (iota((64, 128), 1) >> 3 << 2) + (iota((64, 128), 1) & 3)
    columns = ones_where(iota((64, 128), 0) == r)
    same = (iota((128, 128), 0) >> 6) == ((iota((128, 128), 1) >> 2) & 1)
    w3 = wide(spread(rows, factors_ref[:, :64], columns, same))

    def contract_s(i, xs_ref):
        for g in range(8):
            at = slice(g * 8, g * 8 + 8)
            t = [t_vmem[i % SLOTS, a, at].reshape(256, 64) for a in range(2)]
            th, tl = split(jnp.concatenate(t, 1))
            y = mm(sf[0], jnp.concatenate([th, tl], 1), NN)
            x = y[:, :128] + y[:, 128:] + mm(sf[1], th, NN)
            xs_ref[:, at, :] = x.reshape(16, 8, 128)

    def contract_c(i, xs_ref):
        for k in range(8):
            o = mm_wide(xs_ref[2 * k : 2 * k + 2].reshape(128, 128), w3)
            o = o.T.reshape(16, 8, 128)
            if k < 4:
                own_ref[:, k, i] = o
            else:
                peer_ref[:, k - 4, i] = o

    def two_pairs(step, _):
        i = 2 * step
        copy(i).wait()
        contract_s(i, xa_ref)
        copy(i + 1).wait()
        contract_s(i + 1, xb_ref)
        contract_c(i, xa_ref)
        contract_c(i + 1, xb_ref)
        for out in copies_out(i):
            out.start()

        @pl.when(i + SLOTS < pairs)
        def _():
            copy(i + SLOTS).start()
            copy(i + SLOTS + 1).start()

        return 0

    lax.fori_loop(0, pairs // 2, two_pairs, 0)
    for i in range(0, pairs, 2):
        for out in copies_out(i):
            out.wait()


def core_cut(first, pairs, gz, tensor, factors):
    part = pltpu.HBM((16, 4, pairs, 8, 128), F32)
    return pl.pallas_call(
        functools.partial(core_kernel, first, pairs),
        in_specs=[SMEM, HBM, VMEM],
        out_specs=[HBM, HBM],
        out_shape=[part, part],
        scratch_shapes=[
            pltpu.VMEM((16, 4, pairs, 8, 128), F32),
            pltpu.VMEM((16, 4, pairs, 8, 128), F32),
            pltpu.VMEM((SLOTS, 2, 64, 32, 64), F32),
            pltpu.VMEM((16, 64, 128), F32),
            pltpu.VMEM((16, 64, 128), F32),
            pltpu.SemaphoreType.DMA((SLOTS,)),
            pltpu.SemaphoreType.DMA((2, pairs // 2)),
        ],
        compiler_params=LARGE,
    )(gz, tensor, factors)


def merge_first_kernel(gx_ref, own_ref, other_ref, f2_ref, out_ref):
    rows = 8 * PAIRS[0]
    for g in range(16):
        out_ref[4 * g : 4 * g + 4, :rows] = (own_ref[g] + other_ref[g]).reshape(4, rows, 128)
    f2 = f2_ref[pl.ds(pl.multiple_of(16 * gx_ref[0], 16), 16), :]
    f2 = jnp.concatenate([f2[:8], f2[8:]], 1)
    out_ref[:, 128:] = jnp.broadcast_to(f2[None], (64, 8, 128))


def merge_second_kernel(own_ref, other_ref, sent_ref, out_ref):
    rows = 8 * PAIRS[1]
    for g in range(16):
        total = (own_ref[g] + other_ref[g]).reshape(4, rows, 128)
        out_ref[4 * g : 4 * g + 4, 8 * PAIRS[0] : 128] = total


def merge_first(gx, own, other, f2):
    return pl.pallas_call(
        merge_first_kernel,
        in_specs=[SMEM, VMEM, VMEM, VMEM],
        out_specs=VMEM,
        out_shape=pltpu.VMEM((64, 136, 128), F32),
        compiler_params=PARAMS,
    )(gx, own, other, f2)


def merge_second(own, other, sent):
    return pl.pallas_call(
        merge_second_kernel,
        in_specs=[VMEM, VMEM, VMEM],
        out_specs=VMEM,
        out_shape=pltpu.VMEM((64, 136, 128), F32),
        input_output_aliases={2: 0},
        compiler_params=PARAMS,
    )(own, other, sent)


def first_kernel(c_ref, e_ref, gram_ref, fp_ref, g_ref):
    step = pl.program_id(0)

    @pl.when(step == 0)
    def _():
        fp_ref[...] = jnp.zeros_like(fp_ref)

    low = iota((8, 128), 1) < 64
    total = fp_ref[...]
    for y in range(4):
        top, bottom = [], []
        for x in range(4):
            f2 = c_ref[x, y, 128:]
            turned = pltpu.roll(f2, 64, 1)
            top += [jnp.where(low, f2, 0.0), jnp.where(low, turned, 0.0)]
            bottom += [jnp.where(low, 0.0, turned), jnp.where(low, 0.0, f2)]
        w = wide(split(jnp.concatenate(top + bottom, 0)))
        total += mm_wide(c_ref[:, y, :128].reshape(512, 128), w)
    fp_ref[...] = total

    @pl.when(step == pl.num_programs(0) - 1)
    def _():
        gram, cross = jnp.zeros((128, 128), F32), jnp.zeros((128, 128), F32)
        for r in range(4):
            e = fp_ref[pl.ds(r, 128, stride=4), :]
            e_ref[:, r * 128 : (r + 1) * 128] = e
            eh, el = split(e)
            gram += mm(eh, eh, NT)
            cross += mm(eh, el, NT)
        g_ref[...] = gram + (cross + cross.T)
        group = iota((32, 128), 1) // 32
        rows = [g_ref[pl.ds(i, 32, stride=4), :] for i in range(4)]
        for x in range(4):
            block = jnp.zeros((32, 128), F32)
            for i in range(4):
                moved = pltpu.roll(rows[i], 32 * ((i - x) % 4), 1) if i != x else rows[i]
                block = jnp.where(group == i, moved, block)
            gram_ref[x] = block


def first_gram(c):
    return pl.pallas_call(
        first_kernel,
        grid=(4,),
        in_specs=[
            pl.BlockSpec((4, 4, 136, 128), lambda i: (0, i, 0, 0)),
        ],
        out_specs=[
            pl.BlockSpec((128, 512), lambda i: (0, 0)),
            pl.BlockSpec((4, 32, 128), lambda i: (0, 0, 0)),
        ],
        out_shape=[jax.ShapeDtypeStruct((128, 512), F32), jax.ShapeDtypeStruct((4, 32, 128), F32)],
        scratch_shapes=[pltpu.VMEM((512, 128), F32), pltpu.VMEM((128, 128), F32)],
        compiler_params=PARAMS,
    )(c)


def rows_kernel(parts_ref, f1_ref, out_ref):
    row = jnp.sum(parts_ref[...], axis=0, keepdims=True)
    block = jnp.concatenate([row[:, i * 32 : (i + 1) * 32] for i in range(4)] * 2, 0)
    image = mm_f32(block, f1_ref[...], NN)
    image = jnp.concatenate([image[i : i + 1] for i in range(4)], 1)
    out_ref[...] = jnp.broadcast_to(image[None], out_ref.shape)


def image_rows(parts, f1):
    return pl.pallas_call(
        rows_kernel,
        in_specs=[VMEM, VMEM],
        out_specs=VMEM,
        out_shape=jax.ShapeDtypeStruct((128, 1, 256), F32),
        compiler_params=PARAMS,
    )(parts, f1)


def sum_kernel(parts_ref, out_ref):
    out_ref[...] = jnp.broadcast_to(jnp.sum(parts_ref[...], axis=0, keepdims=True), out_ref.shape)


def sum_for_all(parts):
    return pl.pallas_call(
        sum_kernel,
        in_specs=[VMEM],
        out_specs=VMEM,
        out_shape=jax.ShapeDtypeStruct(parts.shape, F32),
        compiler_params=PARAMS,
    )(parts)


def inverse_factor(normal):
    rows, lanes = iota((64, 128), 0), iota((64, 128), 1)
    m = jnp.concatenate([normal, jnp.where(rows == lanes, 1.0, 0.0)[:, :64].astype(F32)], 1)
    blocks = [m[8 * k : 8 * k + 8] for k in range(8)]
    for k in range(8):
        row = [blocks[k][i : i + 1] for i in range(8)]
        pivot = {}
        for i in range(8):
            for l in range(i, 8):
                entry = blocks[k][i : i + 1, 8 * k + l : 8 * k + l + 1]
                pivot[i, l] = jnp.broadcast_to(entry, (1, 128))
        factor, taken = {}, []
        for i in range(8):
            inverse = 1.0 / pivot[i, i]
            taken.append(row[i] * inverse)
            for l in range(i + 1, 8):
                factor[i, l] = pivot[i, l] * inverse
            for l in range(i + 1, 8):
                row[l] = row[l] - pivot[i, l] * taken[i]
                for n in range(l, 8):
                    pivot[l, n] = pivot[l, n] - factor[i, l] * pivot[i, n]
        for i in reversed(range(8)):
            for l in range(i + 1, 8):
                taken[i] = taken[i] - factor[i, l] * taken[l]
        blocks[k] = jnp.concatenate(row, 0)
        for t in range(k + 1, 8):
            rest = blocks[t]
            for i in range(8):
                at = 8 * k + i
                rest = rest - jnp.broadcast_to(blocks[t][:, at : at + 1], (8, 128)) * taken[i]
            blocks[t] = rest
    m = jnp.concatenate(blocks, 0)
    diagonal = jnp.sum(jnp.where(rows == lanes, m, 0.0), axis=1, keepdims=True)
    return m[:, 64:] * lax.rsqrt(diagonal)


def second_kernel(parts_ref, e_ref, c_ref, new_ref, part_ref, i_ref, y_ref, c_vmem, sem):
    copy = pltpu.make_async_copy(c_ref.at[:, :, pl.ds(0, 128)], c_vmem, sem)
    copy.start()
    rows = jnp.sum(parts_ref[...].reshape(4, 32, 256), axis=0)
    for i in range(4):
        i_ref[pl.ds(i, 32, stride=4), :] = rows[:, i * 64 : (i + 1) * 64]
    image = i_ref[...]
    normal = mm_f32(image, image, TN)
    projected = split(mm_f32(image, e_ref[...], TN))
    inverse = split(inverse_factor(normal))
    basis = mm3(split(image), inverse, NT)
    new_ref[...] = basis * math.sqrt(128)
    y = mm_f32(basis, mm3(inverse, projected, NN), NN)
    for r in range(4):
        y_ref[pl.ds(r, 128, stride=4), :] = y[:, r * 128 : (r + 1) * 128]
    yt = split(y_ref[...].T)
    low = iota((64, 128), 1) < 64
    copy.wait()

    def both(i, _):
        halves = []
        for k in range(2):
            c = split(c_vmem[:, 2 * i + k].reshape(512, 128))
            o = mm3(yt, c, NN)
            halves.append(o[:64, :] + pltpu.roll(o[64:, :], 64, 1))
        part_ref[i] = jnp.where(low, halves[0], pltpu.roll(halves[1], 64, 1))
        return 0

    lax.fori_loop(0, 8, both, 0)


def second_image(parts, e, c):
    return pl.pallas_call(
        second_kernel,
        in_specs=[VMEM, VMEM, HBM],
        out_specs=[VMEM, VMEM],
        out_shape=[jax.ShapeDtypeStruct((128, 64), F32), jax.ShapeDtypeStruct((8, 64, 128), F32)],
        scratch_shapes=[
            pltpu.VMEM((128, 64), F32),
            pltpu.VMEM((512, 128), F32),
            pltpu.VMEM((4, 16, 128, 128), F32),
            pltpu.SemaphoreType.DMA,
        ],
        compiler_params=PARAMS,
    )(parts, e, c)


def last_kernel(at_ref, image_ref, new_ref):
    normal, cross = jnp.zeros((64, 64), F32), jnp.zeros((64, 64), F32)
    for i in range(8):
        h, l = split(image_ref[i])
        normal += mm(h, h, NT)
        cross += mm(h, l, NT)
    inverse = inverse_factor(normal + (cross + cross.T))
    pair = image_ref[at_ref[0]]
    mine = jnp.where(at_ref[1] == 0, pair[:, :64], pair[:, 64:])
    new_ref[...] = mm_f32(mine, inverse, (((0,), (1,)), ((), ()))) * math.sqrt(1024)


def last_factor(at, image):
    return pl.pallas_call(
        last_kernel,
        in_specs=[SMEM, VMEM],
        out_specs=VMEM,
        out_shape=jax.ShapeDtypeStruct((64, 64), F32),
        compiler_params=PARAMS,
    )(at, image)


def to_all(x, names=ALL):
    return lax.all_to_all(x, names, 0, 0, tiled=True)


def swap(x):
    return lax.ppermute(x, "gz", [(0, 1), (1, 0)])


def per_device(tensor, factor_one, factor_two, factor_three, species_factor):
    gx, gy, gz = (lax.axis_index(name).astype(jnp.int32) for name in ALL)

    t = pltpu.with_memory_space_constraint(tensor.transpose(0, 1, 3, 2), pltpu.HBM)
    factors = jnp.concatenate([factor_three, jnp.pad(species_factor.T, ((0, 48), (0, 32)))], 1)
    own_a, peer_a = core_cut(0, PAIRS[0], gz[None], t, factors)
    own_b, peer_b = core_cut(*PAIRS, gz[None], t, factors)
    sent = merge_first(gx[None], own_a, swap(peer_a), factor_two)
    sent = merge_second(own_b, swap(peer_b), sent)
    c = to_all(sent, ("gx", "gy")).reshape(4, 16, 136, 128)

    e, gram = first_gram(c)
    rows = image_rows(to_all(gram.reshape(128, 1, 128)).reshape(128, 128), factor_one)
    new_one, second_part = second_image(to_all(rows).reshape(128, 256), e, c)
    second = to_all(sum_for_all(to_all(second_part.reshape(128, 4, 128)))).reshape(8, 64, 128)
    new_two = last_factor(jnp.stack([gy // 2, gy % 2]), second)
    return lax.dynamic_slice_in_dim(new_one, gx * 32, 32), new_two


def solution(mesh):
    in_specs = (P("gx", "gy", "gz", None), P("gx", None), P("gy", None), P("gz", None), P())
    out_specs = (P("gx", None), P("gy", None))
    return jax.shard_map(
        per_device, mesh=mesh, in_specs=in_specs, out_specs=out_specs, check_vma=False
    )
```

```python
import functools
import math

import jax
import jax.numpy as jnp
from jax import lax
from jax.experimental import pallas as pl
from jax.experimental.pallas import tpu as pltpu
from jax.sharding import PartitionSpec as P

F32, BF16 = jnp.float32, jnp.bfloat16
NN = (((1,), (0,)), ((), ()))
NT = (((1,), (1,)), ((), ()))
TN = (((0,), (0,)), ((), ()))
ALL = ("gx", "gy", "gz")
PAIRS = (12, 4)
SLOTS = 6
VMEM = pl.BlockSpec(memory_space=pltpu.VMEM)
PARAMS = pltpu.CompilerParams(vmem_limit_bytes=12 << 20)
LARGE = pltpu.CompilerParams(vmem_limit_bytes=24 << 20)
HBM = pl.BlockSpec(memory_space=pltpu.HBM)
SMEM = pl.BlockSpec(memory_space=pltpu.SMEM)


def split(x):
    hi = x.astype(BF16)
    return hi, (x - hi.astype(F32)).astype(BF16)


def mm(a, b, dims):
    return lax.dot_general(a, b, dims, preferred_element_type=F32)


def mm3(a, b, dims):
    return mm(a[0], b[0], dims) + (mm(a[0], b[1], dims) + mm(a[1], b[0], dims))


def mm_f32(a, b, dims):
    return mm3(split(a), split(b), dims)


def wide(w):
    zero = jnp.zeros_like(w[0])
    return jnp.concatenate([jnp.concatenate(w, 1), jnp.concatenate([w[0], zero], 1)], 0)


def mm_wide(x, w):
    y = mm(jnp.concatenate(split(x), 1), w, NN)
    return y[:, :128] + y[:, 128:]


def iota(shape, dim):
    return lax.broadcasted_iota(jnp.int32, shape, dim)


def ones_where(mask):
    return jnp.where(mask, 1.0, 0.0).astype(BF16)


def spread(left, x, right, mask):
    return tuple(
        jnp.where(mask, mm(mm(left, part, NN).astype(BF16), right, NN), 0.0).astype(BF16)
        for part in split(x)
    )


def core_kernel(
    first, pairs, gz_ref, t_hbm, factors_ref, own_out, peer_hbm, *scratch
):
    peer_ref, t_vmem, xa_ref, xb_ref, sems, out_sems = scratch[-6:]
    own_ref = scratch[0] if len(scratch) > 6 else own_out

    def copy(i):
        slot = i % SLOTS
        return pltpu.make_async_copy(t_hbm.at[pl.ds(2 * (first + i), 2)], t_vmem.at[slot], sems.at[slot])

    def copies_out(i):
        ends = [(peer_ref, peer_hbm)] + ([(own_ref, own_out)] if len(scratch) > 6 else [])
        return [
            pltpu.make_async_copy(ref.at[:, :, pl.ds(i, 2)], hbm.at[:, :, pl.ds(i, 2)], out_sems.at[k, i // 2])
            for k, (ref, hbm) in enumerate(ends)
        ]

    for i in range(min(SLOTS, pairs)):
        copy(i).start()

    q = ((iota((128, 16), 0) >> 3) + 8 * gz_ref[0]) & 15
    rows = ones_where(q == iota((128, 16), 1))
    columns = ones_where(iota((32, 256), 0) == (iota((32, 256), 1) & 31))
    same = (iota((128, 256), 0) & 7) == (iota((128, 256), 1) >> 5)
    sf = spread(rows, factors_ref[:16, 64:96], columns, same)
    rows = ones_where((iota((128, 64), 0) & 63) == iota((128, 64), 1))
    r = (iota((64, 128), 1) >> 3 << 2) + (iota((64, 128), 1) & 3)
    columns = ones_where(iota((64, 128), 0) == r)
    same = (iota((128, 128), 0) >> 6) == ((iota((128, 128), 1) >> 2) & 1)
    w3 = wide(spread(rows, factors_ref[:, :64], columns, same))

    def contract_s(i, xs_ref):
        for g in range(8):
            at = slice(g * 8, g * 8 + 8)
            t = [t_vmem[i % SLOTS, a, at].reshape(256, 64) for a in range(2)]
            th, tl = split(jnp.concatenate(t, 1))
            y = mm(sf[0], jnp.concatenate([th, tl], 1), NN)
            x = y[:, :128] + y[:, 128:] + mm(sf[1], th, NN)
            xs_ref[:, at, :] = x.reshape(16, 8, 128)

    def contract_c(i, xs_ref):
        for k in range(8):
            o = mm_wide(xs_ref[2 * k : 2 * k + 2].reshape(128, 128), w3)
            o = o.T.reshape(16, 8, 128)
            if k < 4:
                own_ref[:, k, i] = o
            else:
                peer_ref[:, k - 4, i] = o

    def two_pairs(step, _):
        i = 2 * step
        copy(i).wait()
        contract_s(i, xa_ref)
        copy(i + 1).wait()
        contract_s(i + 1, xb_ref)
        contract_c(i, xa_ref)
        contract_c(i + 1, xb_ref)
        for out in copies_out(i):
            out.start()

        @pl.when(i + SLOTS < pairs)
        def _():
            copy(i + SLOTS).start()
            copy(i + SLOTS + 1).start()

        return 0

    lax.fori_loop(0, pairs // 2, two_pairs, 0)
    for i in range(0, pairs, 2):
        for out in copies_out(i):
            out.wait()


def core_cut(first, pairs, gz, tensor, factors):
    shape = (16, 4, pairs, 8, 128)
    stays = first == 0
    return pl.pallas_call(
        functools.partial(core_kernel, first, pairs),
        in_specs=[SMEM, HBM, VMEM],
        out_specs=[VMEM if stays else HBM, HBM],
        out_shape=[(pltpu.VMEM if stays else pltpu.HBM)(shape, F32), pltpu.HBM(shape, F32)],
        scratch_shapes=[pltpu.VMEM(shape, F32)] * (1 if stays else 2)
        + [
            pltpu.VMEM((SLOTS, 2, 64, 32, 64), F32),
            pltpu.VMEM((16, 64, 128), F32),
            pltpu.VMEM((16, 64, 128), F32),
            pltpu.SemaphoreType.DMA((SLOTS,)),
            pltpu.SemaphoreType.DMA((2, pairs // 2)),
        ],
        compiler_params=LARGE,
    )(gz, tensor, factors)


def merge_first_kernel(gx_ref, own_ref, other_ref, f2_ref, out_ref):
    rows = 8 * PAIRS[0]
    for g in range(16):
        out_ref[4 * g : 4 * g + 4, :rows] = (own_ref[g] + other_ref[g]).reshape(4, rows, 128)
    f2 = f2_ref[pl.ds(pl.multiple_of(16 * gx_ref[0], 16), 16), :]
    f2 = jnp.concatenate([f2[:8], f2[8:]], 1)
    out_ref[:, 128:] = jnp.broadcast_to(f2[None], (64, 8, 128))


def merge_second_kernel(own_ref, other_ref, sent_ref, out_ref):
    rows = 8 * PAIRS[1]
    for g in range(16):
        total = (own_ref[g] + other_ref[g]).reshape(4, rows, 128)
        out_ref[4 * g : 4 * g + 4, 8 * PAIRS[0] : 128] = total


def merge_first(gx, own, other, f2):
    return pl.pallas_call(
        merge_first_kernel,
        in_specs=[SMEM, VMEM, VMEM, VMEM],
        out_specs=VMEM,
        out_shape=pltpu.VMEM((64, 136, 128), F32),
        compiler_params=PARAMS,
    )(gx, own, other, f2)


def merge_second(own, other, sent):
    return pl.pallas_call(
        merge_second_kernel,
        in_specs=[VMEM, VMEM, VMEM],
        out_specs=VMEM,
        out_shape=pltpu.VMEM((64, 136, 128), F32),
        input_output_aliases={2: 0},
        compiler_params=PARAMS,
    )(own, other, sent)


def first_kernel(c_ref, e_ref, gram_ref, fp_ref, g_ref):
    low = iota((8, 128), 1) < 64
    total = jnp.zeros((512, 256), F32)
    for y in range(16):
        top, bottom = [], []
        for x in range(4):
            f2 = c_ref[x, y, 128:]
            turned = pltpu.roll(f2, 64, 1)
            top += [jnp.where(low, f2, 0.0), jnp.where(low, turned, 0.0)]
            bottom += [jnp.where(low, 0.0, turned), jnp.where(low, 0.0, f2)]
        w = wide(split(jnp.concatenate(top + bottom, 0)))
        total += mm(jnp.concatenate(split(c_ref[:, y, :128].reshape(512, 128)), 1), w, NN)
    fp_ref[...] = total[:, :128] + total[:, 128:]
    gram, cross = jnp.zeros((128, 128), F32), jnp.zeros((128, 128), F32)
    for r in range(4):
        e = fp_ref[pl.ds(r, 128, stride=4), :]
        e_ref[:, r * 128 : (r + 1) * 128] = e
        eh, el = split(e)
        gram += mm(eh, eh, NT)
        cross += mm(eh, el, NT)
    g_ref[...] = gram + (cross + cross.T)
    group = iota((32, 128), 1) >> 5
    rows = [g_ref[pl.ds(i, 32, stride=4), :] for i in range(4)]
    for x in range(4):
        block = jnp.zeros((32, 128), F32)
        for i in range(4):
            moved = pltpu.roll(rows[i], 32 * ((i - x) % 4), 1) if i != x else rows[i]
            block = jnp.where(group == i, moved, block)
        gram_ref[x] = block


def first_gram(c):
    return pl.pallas_call(
        first_kernel,
        in_specs=[VMEM],
        out_specs=[VMEM, VMEM],
        out_shape=[jax.ShapeDtypeStruct((128, 512), F32), jax.ShapeDtypeStruct((4, 32, 128), F32)],
        scratch_shapes=[pltpu.VMEM((512, 128), F32), pltpu.VMEM((128, 128), F32)],
        compiler_params=PARAMS,
    )(c)


def rows_kernel(parts_ref, f1_ref, out_ref):
    row = jnp.sum(parts_ref[...], axis=0, keepdims=True)
    block = jnp.concatenate([row[:, i * 32 : (i + 1) * 32] for i in range(4)] * 2, 0)
    image = mm_f32(block, f1_ref[...], NN)
    image = jnp.concatenate([image[i : i + 1] for i in range(4)], 1)
    out_ref[...] = jnp.broadcast_to(image[None], out_ref.shape)


def image_rows(parts, f1):
    return pl.pallas_call(
        rows_kernel,
        in_specs=[VMEM, VMEM],
        out_specs=VMEM,
        out_shape=jax.ShapeDtypeStruct((128, 1, 256), F32),
        compiler_params=PARAMS,
    )(parts, f1)


def sum_kernel(parts_ref, out_ref):
    out_ref[...] = jnp.broadcast_to(jnp.sum(parts_ref[...], axis=0, keepdims=True), out_ref.shape)


def sum_for_all(parts):
    return pl.pallas_call(
        sum_kernel,
        in_specs=[VMEM],
        out_specs=VMEM,
        out_shape=jax.ShapeDtypeStruct(parts.shape, F32),
        compiler_params=PARAMS,
    )(parts)


def inverse_factor(normal):
    rows, lanes = iota((64, 128), 0), iota((64, 128), 1)
    m = jnp.concatenate([normal, jnp.where(rows == lanes, 1.0, 0.0)[:, :64].astype(F32)], 1)
    blocks = [m[8 * k : 8 * k + 8] for k in range(8)]
    for k in range(8):
        row = [blocks[k][i : i + 1] for i in range(8)]
        pivot = {}
        for i in range(8):
            for l in range(i, 8):
                entry = blocks[k][i : i + 1, 8 * k + l : 8 * k + l + 1]
                pivot[i, l] = jnp.broadcast_to(entry, (1, 128))
        factor, taken = {}, []
        for i in range(8):
            inverse = 1.0 / pivot[i, i]
            taken.append(row[i] * inverse)
            for l in range(i + 1, 8):
                factor[i, l] = pivot[i, l] * inverse
            for l in range(i + 1, 8):
                row[l] = row[l] - pivot[i, l] * taken[i]
                for n in range(l, 8):
                    pivot[l, n] = pivot[l, n] - factor[i, l] * pivot[i, n]
        for i in reversed(range(8)):
            for l in range(i + 1, 8):
                taken[i] = taken[i] - factor[i, l] * taken[l]
        blocks[k] = jnp.concatenate(row, 0)
        for t in range(k + 1, 8):
            rest = blocks[t]
            for i in range(8):
                at = 8 * k + i
                rest = rest - jnp.broadcast_to(blocks[t][:, at : at + 1], (8, 128)) * taken[i]
            blocks[t] = rest
    m = jnp.concatenate(blocks, 0)
    diagonal = jnp.sum(jnp.where(rows == lanes, m, 0.0), axis=1, keepdims=True)
    return m[:, 64:] * lax.rsqrt(diagonal)


def second_kernel(gx_ref, parts_ref, e_ref, c_ref, new_ref, part_ref, i_ref, y_ref, c_vmem, sem):
    copy = pltpu.make_async_copy(c_ref.at[:, :, pl.ds(0, 128)], c_vmem, sem)
    copy.start()
    rows = jnp.sum(parts_ref[...].reshape(4, 32, 256), axis=0)
    for i in range(4):
        i_ref[pl.ds(i, 32, stride=4), :] = rows[:, i * 64 : (i + 1) * 64]
    image = i_ref[...]
    normal = mm_f32(image, image, TN)
    projected = split(mm_f32(image, e_ref[...], TN))
    inverse = split(inverse_factor(normal))
    basis = mm3(split(image), inverse, NT)
    i_ref[...] = basis * math.sqrt(128)
    new_ref[...] = i_ref[pl.ds(pl.multiple_of(32 * gx_ref[0], 32), 32), :]
    y = mm_f32(basis, mm3(inverse, projected, NN), NN)
    for r in range(4):
        y_ref[pl.ds(r, 128, stride=4), :] = y[:, r * 128 : (r + 1) * 128]
    yt = split(y_ref[...].T)
    both = jnp.concatenate(yt, 0)
    low = iota((64, 128), 1) < 64
    copy.wait()

    def two(i, _):
        c = [c_vmem[:, 2 * i + k].reshape(512, 128) for k in range(2)]
        ch, cl = split(jnp.concatenate(c, 1))
        o = mm(both, ch, NN)
        o = o[:128] + o[128:] + mm(yt[0], cl, NN)
        halves = [o[:64, at : at + 128] + pltpu.roll(o[64:, at : at + 128], 64, 1) for at in (0, 128)]
        part_ref[i] = jnp.where(low, halves[0], pltpu.roll(halves[1], 64, 1))
        return 0

    lax.fori_loop(0, 8, two, 0, unroll=True)


def second_image(gx, parts, e, c):
    return pl.pallas_call(
        second_kernel,
        in_specs=[SMEM, VMEM, VMEM, HBM],
        out_specs=[VMEM, VMEM],
        out_shape=[jax.ShapeDtypeStruct((32, 64), F32), jax.ShapeDtypeStruct((8, 64, 128), F32)],
        scratch_shapes=[
            pltpu.VMEM((128, 64), F32),
            pltpu.VMEM((512, 128), F32),
            pltpu.VMEM((4, 16, 128, 128), F32),
            pltpu.SemaphoreType.DMA,
        ],
        compiler_params=PARAMS,
    )(gx, parts, e, c)


def last_kernel(at_ref, image_ref, new_ref):
    normal, cross = jnp.zeros((64, 64), F32), jnp.zeros((64, 64), F32)
    for i in range(8):
        h, l = split(image_ref[i])
        normal += mm(h, h, NT)
        cross += mm(h, l, NT)
    inverse = inverse_factor(normal + (cross + cross.T))
    pair = image_ref[at_ref[0]]
    mine = jnp.where(at_ref[1] == 0, pair[:, :64], pair[:, 64:])
    new_ref[...] = mm_f32(mine, inverse, (((0,), (1,)), ((), ()))) * math.sqrt(1024)


def last_factor(at, image):
    return pl.pallas_call(
        last_kernel,
        in_specs=[SMEM, VMEM],
        out_specs=VMEM,
        out_shape=jax.ShapeDtypeStruct((64, 64), F32),
        compiler_params=PARAMS,
    )(at, image)


def to_all(x, names=ALL):
    return lax.all_to_all(x, names, 0, 0, tiled=True)


def in_hbm(x):
    return pltpu.with_memory_space_constraint(x, pltpu.HBM)


def swap(x):
    return lax.ppermute(x, "gz", [(0, 1), (1, 0)])


def per_device(tensor, factor_one, factor_two, factor_three, species_factor):
    gx, gy, gz = (lax.axis_index(name).astype(jnp.int32) for name in ALL)

    t = in_hbm(tensor.transpose(0, 1, 3, 2))
    factors = jnp.concatenate([factor_three, jnp.pad(species_factor.T, ((0, 48), (0, 32)))], 1)
    own_a, peer_a = core_cut(0, PAIRS[0], gz[None], t, factors)
    own_b, peer_b = core_cut(*PAIRS, gz[None], t, factors)
    sent = merge_first(gx[None], own_a, swap(peer_a), factor_two)
    sent = merge_second(own_b, swap(peer_b), sent)
    c = to_all(sent, ("gx", "gy")).reshape(4, 16, 136, 128)

    e, gram = first_gram(c)
    rows = image_rows(to_all(gram.reshape(128, 1, 128)).reshape(128, 128), factor_one)
    new_one, second_part = second_image(gx[None], to_all(rows).reshape(128, 256), e, c)
    second = to_all(sum_for_all(to_all(second_part.reshape(128, 4, 128)))).reshape(8, 64, 128)
    new_two = last_factor(jnp.stack([gy // 2, gy % 2]), second)
    return new_one, new_two


def solution(mesh):
    in_specs = (P("gx", "gy", "gz", None), P("gx", None), P("gy", None), P("gz", None), P())
    out_specs = (P("gx", None), P("gy", None))
    return jax.shard_map(
        per_device, mesh=mesh, in_specs=in_specs, out_specs=out_specs, check_vma=False
    )
```

```python
import functools
import math

import jax
import jax.numpy as jnp
from jax import lax
from jax.experimental import pallas as pl
from jax.experimental.pallas import tpu as pltpu
from jax.sharding import PartitionSpec as P

F32, BF16 = jnp.float32, jnp.bfloat16
NN = (((1,), (0,)), ((), ()))
NT = (((1,), (1,)), ((), ()))
TN = (((0,), (0,)), ((), ()))
ALL = ("gx", "gy", "gz")
PAIRS = (12, 4)
SLOTS = 6
VMEM = pl.BlockSpec(memory_space=pltpu.VMEM)
PARAMS = pltpu.CompilerParams(vmem_limit_bytes=12 << 20)
LARGE = pltpu.CompilerParams(vmem_limit_bytes=28 << 20)
HBM = pl.BlockSpec(memory_space=pltpu.HBM)
SMEM = pl.BlockSpec(memory_space=pltpu.SMEM)


def split(x):
    hi = x.astype(BF16)
    return hi, (x - hi.astype(F32)).astype(BF16)


def mm(a, b, dims):
    return lax.dot_general(a, b, dims, preferred_element_type=F32)


def mm3(a, b, dims):
    return mm(a[0], b[0], dims) + (mm(a[0], b[1], dims) + mm(a[1], b[0], dims))


def mm_f32(a, b, dims):
    return mm3(split(a), split(b), dims)


def wide(w):
    zero = jnp.zeros_like(w[0])
    return jnp.concatenate([jnp.concatenate(w, 1), jnp.concatenate([w[0], zero], 1)], 0)


def mm_wide(x, w):
    y = mm(jnp.concatenate(split(x), 1), w, NN)
    return y[:, :128] + y[:, 128:]


def iota(shape, dim):
    return lax.broadcasted_iota(jnp.int32, shape, dim)


def ones_where(mask):
    return jnp.where(mask, 1.0, 0.0).astype(BF16)


def spread(left, x, right, mask):
    return tuple(
        jnp.where(mask, mm(mm(left, part, NN).astype(BF16), right, NN), 0.0).astype(BF16)
        for part in split(x)
    )


def core_kernel(chunk, gz_ref, t_hbm, factors_ref, *rest):
    first, pairs = (0, PAIRS[0]) if chunk == 0 else PAIRS
    if chunk == 0:
        own_out, peer_hbm, ready_ref, *scratch = rest
        own_ref = own_out
    else:
        ready_ref, own_out, peer_hbm, own_ref, *scratch = rest
    peer_ref, t_vmem, xa_ref, xb_ref, sems, out_sems, ready_sem = scratch
    skip = 2 * chunk

    def copy(i):
        slot = i % SLOTS
        return pltpu.make_async_copy(t_hbm.at[pl.ds(2 * (first + i), 2)], t_vmem.at[slot], sems.at[slot])

    def copy_ready():
        return pltpu.make_async_copy(t_hbm.at[pl.ds(2 * PAIRS[0], 4)], ready_ref, ready_sem)

    def copies_out(i):
        ends = [(peer_ref, peer_hbm)] + ([(own_ref, own_out)] if chunk == 1 else [])
        return [
            pltpu.make_async_copy(ref.at[:, :, pl.ds(i, 2)], hbm.at[:, :, pl.ds(i, 2)], out_sems.at[k, i // 2])
            for k, (ref, hbm) in enumerate(ends)
        ]

    for i in range(skip, min(SLOTS, pairs)):
        copy(i).start()

    q = ((iota((128, 16), 0) >> 3) + 8 * gz_ref[0]) & 15
    rows = ones_where(q == iota((128, 16), 1))
    columns = ones_where(iota((32, 256), 0) == (iota((32, 256), 1) & 31))
    same = (iota((128, 256), 0) & 7) == (iota((128, 256), 1) >> 5)
    sf = spread(rows, factors_ref[:16, 64:96], columns, same)
    rows = ones_where((iota((128, 64), 0) & 63) == iota((128, 64), 1))
    r = (iota((64, 128), 1) >> 3 << 2) + (iota((64, 128), 1) & 3)
    columns = ones_where(iota((64, 128), 0) == r)
    same = (iota((128, 128), 0) >> 6) == ((iota((128, 128), 1) >> 2) & 1)
    w3 = wide(spread(rows, factors_ref[:, :64], columns, same))

    def contract_s(t_ref, xs_ref):
        for g in range(8):
            at = slice(g * 8, g * 8 + 8)
            th, tl = split(jnp.concatenate([t_ref[a, at].reshape(256, 64) for a in range(2)], 1))
            y = mm(sf[0], jnp.concatenate([th, tl], 1), NN)
            x = y[:, :128] + y[:, 128:] + mm(sf[1], th, NN)
            xs_ref[:, at, :] = x.reshape(16, 8, 128)

    def contract_c(i, xs_ref):
        for k in range(8):
            o = mm_wide(xs_ref[2 * k : 2 * k + 2].reshape(128, 128), w3)
            o = o.T.reshape(16, 8, 128)
            if k < 4:
                own_ref[:, k, i] = o
            else:
                peer_ref[:, k - 4, i] = o

    def finish(i):
        contract_c(i, xa_ref)
        contract_c(i + 1, xb_ref)
        for out in copies_out(i):
            out.start()

    def two_pairs(step, _):
        i = 2 * step
        copy(i).wait()
        contract_s(t_vmem.at[i % SLOTS], xa_ref)
        copy(i + 1).wait()
        contract_s(t_vmem.at[(i + 1) % SLOTS], xb_ref)
        finish(i)

        @pl.when(i + SLOTS < pairs)
        def _():
            copy(i + SLOTS).start()
            copy(i + SLOTS + 1).start()

        if chunk == 0:

            @pl.when(i + SLOTS == pairs)
            def _():
                copy_ready().start()

        return 0

    if chunk == 1:
        contract_s(ready_ref.at[pl.ds(0, 2)], xa_ref)
        contract_s(ready_ref.at[pl.ds(2, 2)], xb_ref)
        finish(0)
    lax.fori_loop(chunk, pairs // 2, two_pairs, 0)
    for i in range(0, pairs, 2):
        for out in copies_out(i):
            out.wait()
    if chunk == 0:
        copy_ready().wait()


def core_cut(chunk, gz, tensor, factors, *ready):
    pairs = PAIRS[chunk]
    shape, fetched = (16, 4, pairs, 8, 128), (4, 64, 32, 64)
    peer = pltpu.HBM(shape, F32)
    if chunk == 0:
        out_specs, out_shape = [VMEM, HBM, VMEM], [pltpu.VMEM(shape, F32), peer, pltpu.VMEM(fetched, F32)]
    else:
        out_specs, out_shape = [HBM, HBM], [peer, peer]
    return pl.pallas_call(
        functools.partial(core_kernel, chunk),
        in_specs=[SMEM, HBM, VMEM] + [VMEM] * chunk,
        out_specs=out_specs,
        out_shape=out_shape,
        scratch_shapes=[pltpu.VMEM(shape, F32)] * (1 + chunk)
        + [
            pltpu.VMEM((SLOTS, 2, 64, 32, 64), F32),
            pltpu.VMEM((16, 64, 128), F32),
            pltpu.VMEM((16, 64, 128), F32),
            pltpu.SemaphoreType.DMA((SLOTS,)),
            pltpu.SemaphoreType.DMA((2, pairs // 2)),
            pltpu.SemaphoreType.DMA,
        ],
        compiler_params=LARGE,
    )(gz, tensor, factors, *ready)


def merge_first_kernel(gx_ref, own_ref, other_hbm, f2_ref, out_ref, other_ref, sems):
    rows = 8 * PAIRS[0]
    copies = [
        pltpu.make_async_copy(other_hbm.at[pl.ds(2 * g, 2)], other_ref.at[pl.ds(2 * g, 2)], sems.at[g])
        for g in range(8)
    ]
    for copy in copies:
        copy.start()
    f2 = f2_ref[pl.ds(pl.multiple_of(16 * gx_ref[0], 16), 16), :]
    f2 = jnp.concatenate([f2[:8], f2[8:]], 1)
    out_ref[:, 128:] = jnp.broadcast_to(f2[None], (64, 8, 128))
    for g in range(16):
        if g % 2 == 0:
            copies[g // 2].wait()
        out_ref[4 * g : 4 * g + 4, :rows] = (own_ref[g] + other_ref[g]).reshape(4, rows, 128)


def merge_second_kernel(own_ref, other_ref, sent_ref, out_ref):
    rows = 8 * PAIRS[1]
    for g in range(16):
        total = (own_ref[g] + other_ref[g]).reshape(4, rows, 128)
        out_ref[4 * g : 4 * g + 4, 8 * PAIRS[0] : 128] = total


def merge_first(gx, own, other, f2):
    return pl.pallas_call(
        merge_first_kernel,
        in_specs=[SMEM, VMEM, HBM, VMEM],
        out_specs=VMEM,
        out_shape=pltpu.VMEM((64, 136, 128), F32),
        scratch_shapes=[pltpu.VMEM(own.shape, F32), pltpu.SemaphoreType.DMA((8,))],
        compiler_params=PARAMS,
    )(gx, own, in_hbm(other), f2)


def merge_second(own, other, sent):
    return pl.pallas_call(
        merge_second_kernel,
        in_specs=[VMEM, VMEM, VMEM],
        out_specs=VMEM,
        out_shape=pltpu.VMEM((64, 136, 128), F32),
        input_output_aliases={2: 0},
        compiler_params=PARAMS,
    )(own, other, sent)


def first_kernel(c_ref, e_ref, gram_ref, fp_ref, g_ref):
    low = iota((8, 128), 1) < 64
    total = jnp.zeros((512, 256), F32)
    for y in range(16):
        top, bottom = [], []
        for x in range(4):
            f2 = c_ref[x, y, 128:]
            turned = pltpu.roll(f2, 64, 1)
            top += [jnp.where(low, f2, 0.0), jnp.where(low, turned, 0.0)]
            bottom += [jnp.where(low, 0.0, turned), jnp.where(low, 0.0, f2)]
        w = wide(split(jnp.concatenate(top + bottom, 0)))
        total += mm(jnp.concatenate(split(c_ref[:, y, :128].reshape(512, 128)), 1), w, NN)
    fp_ref[...] = total[:, :128] + total[:, 128:]
    gram, cross = jnp.zeros((128, 128), F32), jnp.zeros((128, 128), F32)
    for r in range(4):
        e = fp_ref[pl.ds(r, 128, stride=4), :]
        e_ref[:, r * 128 : (r + 1) * 128] = e
        eh, el = split(e)
        gram += mm(eh, eh, NT)
        cross += mm(eh, el, NT)
    g_ref[...] = gram + (cross + cross.T)
    group = iota((32, 128), 1) >> 5
    rows = [g_ref[pl.ds(i, 32, stride=4), :] for i in range(4)]
    for x in range(4):
        block = jnp.zeros((32, 128), F32)
        for i in range(4):
            moved = pltpu.roll(rows[i], 32 * ((i - x) % 4), 1) if i != x else rows[i]
            block = jnp.where(group == i, moved, block)
        gram_ref[x] = block


def first_gram(c):
    return pl.pallas_call(
        first_kernel,
        in_specs=[VMEM],
        out_specs=[VMEM, VMEM],
        out_shape=[jax.ShapeDtypeStruct((128, 512), F32), jax.ShapeDtypeStruct((4, 32, 128), F32)],
        scratch_shapes=[pltpu.VMEM((512, 128), F32), pltpu.VMEM((128, 128), F32)],
        compiler_params=PARAMS,
    )(c)


def rows_kernel(parts_ref, f1_ref, out_ref):
    row = jnp.sum(parts_ref[...], axis=0, keepdims=True)
    block = jnp.concatenate([row[:, i * 32 : (i + 1) * 32] for i in range(4)] * 2, 0)
    image = mm_f32(block, f1_ref[...], NN)
    image = jnp.concatenate([image[i : i + 1] for i in range(4)], 1)
    out_ref[...] = jnp.broadcast_to(image[None], out_ref.shape)


def image_rows(parts, f1):
    return pl.pallas_call(
        rows_kernel,
        in_specs=[VMEM, VMEM],
        out_specs=VMEM,
        out_shape=jax.ShapeDtypeStruct((128, 1, 256), F32),
        compiler_params=PARAMS,
    )(parts, f1)


def sum_kernel(parts_ref, out_ref):
    out_ref[...] = jnp.broadcast_to(jnp.sum(parts_ref[...], axis=0, keepdims=True), out_ref.shape)


def sum_for_all(parts):
    return pl.pallas_call(
        sum_kernel,
        in_specs=[VMEM],
        out_specs=VMEM,
        out_shape=jax.ShapeDtypeStruct(parts.shape, F32),
        compiler_params=PARAMS,
    )(parts)


def inverse_factor(normal):
    rows, lanes = iota((64, 128), 0), iota((64, 128), 1)
    m = jnp.concatenate([normal, jnp.where(rows == lanes, 1.0, 0.0)[:, :64].astype(F32)], 1)
    blocks = [m[8 * k : 8 * k + 8] for k in range(8)]
    for k in range(8):
        row = [blocks[k][i : i + 1] for i in range(8)]
        pivot = {}
        for i in range(8):
            for l in range(i, 8):
                entry = blocks[k][i : i + 1, 8 * k + l : 8 * k + l + 1]
                pivot[i, l] = jnp.broadcast_to(entry, (1, 128))
        factor, taken = {}, []
        for i in range(8):
            inverse = 1.0 / pivot[i, i]
            taken.append(row[i] * inverse)
            for l in range(i + 1, 8):
                factor[i, l] = pivot[i, l] * inverse
            for l in range(i + 1, 8):
                row[l] = row[l] - pivot[i, l] * taken[i]
                for n in range(l, 8):
                    pivot[l, n] = pivot[l, n] - factor[i, l] * pivot[i, n]
        for i in reversed(range(8)):
            for l in range(i + 1, 8):
                taken[i] = taken[i] - factor[i, l] * taken[l]
        blocks[k] = jnp.concatenate(row, 0)
        for t in range(k + 1, 8):
            rest = blocks[t]
            for i in range(8):
                at = 8 * k + i
                rest = rest - jnp.broadcast_to(blocks[t][:, at : at + 1], (8, 128)) * taken[i]
            blocks[t] = rest
    m = jnp.concatenate(blocks, 0)
    diagonal = jnp.sum(jnp.where(rows == lanes, m, 0.0), axis=1, keepdims=True)
    return m[:, 64:] * lax.rsqrt(diagonal)


def second_kernel(gx_ref, parts_ref, e_ref, c_ref, new_ref, part_ref, i_ref, y_ref, c_vmem, sem):
    copy = pltpu.make_async_copy(c_ref.at[:, :, pl.ds(0, 128)], c_vmem, sem)
    copy.start()
    rows = jnp.sum(parts_ref[...].reshape(4, 32, 256), axis=0)
    for i in range(4):
        i_ref[pl.ds(i, 32, stride=4), :] = rows[:, i * 64 : (i + 1) * 64]
    image = i_ref[...]
    normal = mm_f32(image, image, TN)
    projected = split(mm_f32(image, e_ref[...], TN))
    inverse = split(inverse_factor(normal))
    basis = mm3(split(image), inverse, NT)
    i_ref[...] = basis * math.sqrt(128)
    new_ref[...] = i_ref[pl.ds(pl.multiple_of(32 * gx_ref[0], 32), 32), :]
    y = mm_f32(basis, mm3(inverse, projected, NN), NN)
    for r in range(4):
        y_ref[pl.ds(r, 128, stride=4), :] = y[:, r * 128 : (r + 1) * 128]
    yt = split(y_ref[...].T)
    both = jnp.concatenate(yt, 0)
    low = iota((64, 128), 1) < 64
    copy.wait()

    def two(i, _):
        c = [c_vmem[:, 2 * i + k].reshape(512, 128) for k in range(2)]
        ch, cl = split(jnp.concatenate(c, 1))
        o = mm(both, ch, NN)
        o = o[:128] + o[128:] + mm(yt[0], cl, NN)
        halves = [o[:64, at : at + 128] + pltpu.roll(o[64:, at : at + 128], 64, 1) for at in (0, 128)]
        part_ref[i] = jnp.where(low, halves[0], pltpu.roll(halves[1], 64, 1))
        return 0

    lax.fori_loop(0, 8, two, 0, unroll=True)


def second_image(gx, parts, e, c):
    return pl.pallas_call(
        second_kernel,
        in_specs=[SMEM, VMEM, VMEM, HBM],
        out_specs=[VMEM, VMEM],
        out_shape=[jax.ShapeDtypeStruct((32, 64), F32), jax.ShapeDtypeStruct((8, 64, 128), F32)],
        scratch_shapes=[
            pltpu.VMEM((128, 64), F32),
            pltpu.VMEM((512, 128), F32),
            pltpu.VMEM((4, 16, 128, 128), F32),
            pltpu.SemaphoreType.DMA,
        ],
        compiler_params=PARAMS,
    )(gx, parts, e, c)


def last_kernel(at_ref, image_ref, new_ref):
    normal, cross = jnp.zeros((64, 64), F32), jnp.zeros((64, 64), F32)
    for i in range(8):
        h, l = split(image_ref[i])
        normal += mm(h, h, NT)
        cross += mm(h, l, NT)
    inverse = inverse_factor(normal + (cross + cross.T))
    pair = image_ref[at_ref[0]]
    mine = jnp.where(at_ref[1] == 0, pair[:, :64], pair[:, 64:])
    new_ref[...] = mm_f32(mine, inverse, (((0,), (1,)), ((), ()))) * math.sqrt(1024)


def last_factor(at, image):
    return pl.pallas_call(
        last_kernel,
        in_specs=[SMEM, VMEM],
        out_specs=VMEM,
        out_shape=jax.ShapeDtypeStruct((64, 64), F32),
        compiler_params=PARAMS,
    )(at, image)


def to_all(x, names=ALL):
    return lax.all_to_all(x, names, 0, 0, tiled=True)


def in_hbm(x):
    return pltpu.with_memory_space_constraint(x, pltpu.HBM)


def swap(x):
    return lax.ppermute(x, "gz", [(0, 1), (1, 0)])


def per_device(tensor, factor_one, factor_two, factor_three, species_factor):
    gx, gy, gz = (lax.axis_index(name).astype(jnp.int32) for name in ALL)

    t = in_hbm(tensor.transpose(0, 1, 3, 2))
    factors = jnp.concatenate([factor_three, jnp.pad(species_factor.T, ((0, 48), (0, 32)))], 1)
    own_a, peer_a, ready = core_cut(0, gz[None], t, factors)
    own_b, peer_b = core_cut(1, gz[None], t, factors, ready)
    sent = merge_first(gx[None], own_a, swap(peer_a), factor_two)
    sent = merge_second(own_b, swap(peer_b), sent)
    c = to_all(sent, ("gx", "gy")).reshape(4, 16, 136, 128)

    e, gram = first_gram(c)
    rows = image_rows(to_all(gram.reshape(128, 1, 128)).reshape(128, 128), factor_one)
    new_one, second_part = second_image(gx[None], to_all(rows).reshape(128, 256), e, c)
    second = to_all(sum_for_all(to_all(second_part.reshape(128, 4, 128)))).reshape(8, 64, 128)
    new_two = last_factor(jnp.stack([gy // 2, gy % 2]), second)
    return new_one, new_two


def solution(mesh):
    in_specs = (P("gx", "gy", "gz", None), P("gx", None), P("gy", None), P("gz", None), P())
    out_specs = (P("gx", None), P("gy", None))
    return jax.shard_map(
        per_device, mesh=mesh, in_specs=in_specs, out_specs=out_specs, check_vma=False
    )
```

```python
import functools
import math

import jax
import jax.numpy as jnp
from jax import lax
from jax.experimental import pallas as pl
from jax.experimental.pallas import tpu as pltpu
from jax.sharding import PartitionSpec as P

F32, BF16 = jnp.float32, jnp.bfloat16
NN = (((1,), (0,)), ((), ()))
NT = (((1,), (1,)), ((), ()))
TN = (((0,), (0,)), ((), ()))
ALL = ("gx", "gy", "gz")
PAIRS = (12, 4)
SLOTS = 6
VMEM = pl.BlockSpec(memory_space=pltpu.VMEM)
PARAMS = pltpu.CompilerParams(vmem_limit_bytes=12 << 20)
LARGE = pltpu.CompilerParams(vmem_limit_bytes=28 << 20)
HBM = pl.BlockSpec(memory_space=pltpu.HBM)
SMEM = pl.BlockSpec(memory_space=pltpu.SMEM)


def split(x):
    hi = x.astype(BF16)
    return hi, (x - hi.astype(F32)).astype(BF16)


def mm(a, b, dims):
    return lax.dot_general(a, b, dims, preferred_element_type=F32)


def mm3(a, b, dims):
    return mm(a[0], b[0], dims) + (mm(a[0], b[1], dims) + mm(a[1], b[0], dims))


def mm_f32(a, b, dims):
    return mm3(split(a), split(b), dims)


def mm_exact(a, b, dims):
    return lax.dot_general(a, b, dims, precision=lax.Precision.HIGHEST, preferred_element_type=F32)


def wide(w):
    zero = jnp.zeros_like(w[0])
    return jnp.concatenate([jnp.concatenate(w, 1), jnp.concatenate([w[0], zero], 1)], 0)


def mm_wide(x, w):
    y = mm(jnp.concatenate(split(x), 1), w, NN)
    return y[:, :128] + y[:, 128:]


def iota(shape, dim):
    return lax.broadcasted_iota(jnp.int32, shape, dim)


def ones_where(mask):
    return jnp.where(mask, 1.0, 0.0).astype(BF16)


def spread(left, x, right, mask):
    return tuple(
        jnp.where(mask, mm(mm(left, part, NN).astype(BF16), right, NN), 0.0).astype(BF16)
        for part in split(x)
    )


def core_kernel(chunk, gz_ref, t_hbm, factors_ref, *rest):
    first, pairs = (0, PAIRS[0]) if chunk == 0 else PAIRS
    if chunk == 0:
        own_out, peer_hbm, ready_ref, *scratch = rest
        own_ref = own_out
    else:
        ready_ref, own_out, peer_hbm, own_ref, *scratch = rest
    peer_ref, t_vmem, xa_ref, xb_ref, sems, out_sems, ready_sem = scratch
    skip = 2 * chunk

    def copy(i):
        slot = i % SLOTS
        return pltpu.make_async_copy(t_hbm.at[pl.ds(2 * (first + i), 2)], t_vmem.at[slot], sems.at[slot])

    def copy_ready():
        return pltpu.make_async_copy(t_hbm.at[pl.ds(2 * PAIRS[0], 4)], ready_ref, ready_sem)

    def copies_out(i):
        ends = [(peer_ref, peer_hbm)] + ([(own_ref, own_out)] if chunk == 1 else [])
        return [
            pltpu.make_async_copy(ref.at[:, :, pl.ds(i, 2)], hbm.at[:, :, pl.ds(i, 2)], out_sems.at[k, i // 2])
            for k, (ref, hbm) in enumerate(ends)
        ]

    for i in range(skip, min(SLOTS, pairs)):
        copy(i).start()

    q = ((iota((128, 16), 0) >> 3) + 8 * gz_ref[0]) & 15
    rows = ones_where(q == iota((128, 16), 1))
    columns = ones_where(iota((32, 256), 0) == (iota((32, 256), 1) & 31))
    same = (iota((128, 256), 0) & 7) == (iota((128, 256), 1) >> 5)
    sf = spread(rows, factors_ref[:16, 64:96], columns, same)
    rows = ones_where((iota((128, 64), 0) & 63) == iota((128, 64), 1))
    r = (iota((64, 128), 1) >> 3 << 2) + (iota((64, 128), 1) & 3)
    columns = ones_where(iota((64, 128), 0) == r)
    same = (iota((128, 128), 0) >> 6) == ((iota((128, 128), 1) >> 2) & 1)
    w3 = wide(spread(rows, factors_ref[:, :64], columns, same))

    def contract_s(t_ref, xs_ref):
        for g in range(8):
            at = slice(g * 8, g * 8 + 8)
            th, tl = split(jnp.concatenate([t_ref[a, at].reshape(256, 64) for a in range(2)], 1))
            y = mm(sf[0], jnp.concatenate([th, tl], 1), NN)
            x = y[:, :128] + y[:, 128:] + mm(sf[1], th, NN)
            xs_ref[:, at, :] = x.reshape(16, 8, 128)

    def contract_c(i, xs_ref):
        for k in range(8):
            o = mm_wide(xs_ref[2 * k : 2 * k + 2].reshape(128, 128), w3)
            o = o.T.reshape(16, 8, 128)
            if k < 4:
                own_ref[:, k, i] = o
            else:
                peer_ref[:, k - 4, i] = o

    def finish(i):
        contract_c(i, xa_ref)
        contract_c(i + 1, xb_ref)
        for out in copies_out(i):
            out.start()

    def two_pairs(step, _):
        i = 2 * step
        copy(i).wait()
        contract_s(t_vmem.at[i % SLOTS], xa_ref)
        copy(i + 1).wait()
        contract_s(t_vmem.at[(i + 1) % SLOTS], xb_ref)
        finish(i)

        @pl.when(i + SLOTS < pairs)
        def _():
            copy(i + SLOTS).start()
            copy(i + SLOTS + 1).start()

        if chunk == 0:

            @pl.when(i + SLOTS == pairs)
            def _():
                copy_ready().start()

        return 0

    if chunk == 1:
        contract_s(ready_ref.at[pl.ds(0, 2)], xa_ref)
        contract_s(ready_ref.at[pl.ds(2, 2)], xb_ref)
        finish(0)
    lax.fori_loop(chunk, pairs // 2, two_pairs, 0)
    for i in range(0, pairs, 2):
        for out in copies_out(i):
            out.wait()
    if chunk == 0:
        copy_ready().wait()


def core_cut(chunk, gz, tensor, factors, *ready):
    pairs = PAIRS[chunk]
    shape, fetched = (16, 4, pairs, 8, 128), (4, 64, 32, 64)
    peer = pltpu.HBM(shape, F32)
    if chunk == 0:
        out_specs, out_shape = [VMEM, HBM, VMEM], [pltpu.VMEM(shape, F32), peer, pltpu.VMEM(fetched, F32)]
    else:
        out_specs, out_shape = [HBM, HBM], [peer, peer]
    return pl.pallas_call(
        functools.partial(core_kernel, chunk),
        in_specs=[SMEM, HBM, VMEM] + [VMEM] * chunk,
        out_specs=out_specs,
        out_shape=out_shape,
        scratch_shapes=[pltpu.VMEM(shape, F32)] * (1 + chunk)
        + [
            pltpu.VMEM((SLOTS, 2, 64, 32, 64), F32),
            pltpu.VMEM((16, 64, 128), F32),
            pltpu.VMEM((16, 64, 128), F32),
            pltpu.SemaphoreType.DMA((SLOTS,)),
            pltpu.SemaphoreType.DMA((2, pairs // 2)),
            pltpu.SemaphoreType.DMA,
        ],
        compiler_params=LARGE,
    )(gz, tensor, factors, *ready)


def merge_first_kernel(gx_ref, own_ref, other_hbm, f2_ref, out_ref, other_ref, sems):
    rows = 8 * PAIRS[0]
    copies = [
        pltpu.make_async_copy(other_hbm.at[pl.ds(2 * g, 2)], other_ref.at[pl.ds(2 * g, 2)], sems.at[g])
        for g in range(8)
    ]
    for copy in copies:
        copy.start()
    f2 = f2_ref[pl.ds(pl.multiple_of(16 * gx_ref[0], 16), 16), :]
    f2 = jnp.concatenate([f2[:8], f2[8:]], 1)
    out_ref[:, 128:] = jnp.broadcast_to(f2[None], (64, 8, 128))
    for g in range(16):
        if g % 2 == 0:
            copies[g // 2].wait()
        out_ref[4 * g : 4 * g + 4, :rows] = (own_ref[g] + other_ref[g]).reshape(4, rows, 128)


def merge_second_kernel(own_ref, other_ref, sent_ref, out_ref):
    rows = 8 * PAIRS[1]
    for g in range(16):
        total = (own_ref[g] + other_ref[g]).reshape(4, rows, 128)
        out_ref[4 * g : 4 * g + 4, 8 * PAIRS[0] : 128] = total


def merge_first(gx, own, other, f2):
    return pl.pallas_call(
        merge_first_kernel,
        in_specs=[SMEM, VMEM, HBM, VMEM],
        out_specs=VMEM,
        out_shape=pltpu.VMEM((64, 136, 128), F32),
        scratch_shapes=[pltpu.VMEM(own.shape, F32), pltpu.SemaphoreType.DMA((8,))],
        compiler_params=PARAMS,
    )(gx, own, in_hbm(other), f2)


def merge_second(own, other, sent):
    return pl.pallas_call(
        merge_second_kernel,
        in_specs=[VMEM, VMEM, VMEM],
        out_specs=VMEM,
        out_shape=pltpu.VMEM((64, 136, 128), F32),
        input_output_aliases={2: 0},
        compiler_params=PARAMS,
    )(own, other, sent)


def first_kernel(c_ref, e_ref, gram_ref, fp_ref, g_ref):
    low = iota((8, 128), 1) < 64
    total = jnp.zeros((512, 256), F32)
    for y in range(16):
        top, bottom = [], []
        for x in range(4):
            f2 = c_ref[x, y, 128:]
            turned = pltpu.roll(f2, 64, 1)
            top += [jnp.where(low, f2, 0.0), jnp.where(low, turned, 0.0)]
            bottom += [jnp.where(low, 0.0, turned), jnp.where(low, 0.0, f2)]
        w = wide(split(jnp.concatenate(top + bottom, 0)))
        total += mm(jnp.concatenate(split(c_ref[:, y, :128].reshape(512, 128)), 1), w, NN)
    fp_ref[...] = total[:, :128] + total[:, 128:]
    gram, cross = jnp.zeros((128, 128), F32), jnp.zeros((128, 128), F32)
    for r in range(4):
        e = fp_ref[pl.ds(r, 128, stride=4), :]
        e_ref[:, r * 128 : (r + 1) * 128] = e
        eh, el = split(e)
        gram += mm(eh, eh, NT) + mm(el, el, NT)
        cross += mm(eh, el, NT)
    g_ref[...] = gram + (cross + cross.T)
    group = iota((32, 128), 1) >> 5
    rows = [g_ref[pl.ds(i, 32, stride=4), :] for i in range(4)]
    for x in range(4):
        block = jnp.zeros((32, 128), F32)
        for i in range(4):
            moved = pltpu.roll(rows[i], 32 * ((i - x) % 4), 1) if i != x else rows[i]
            block = jnp.where(group == i, moved, block)
        gram_ref[x] = block


def first_gram(c):
    return pl.pallas_call(
        first_kernel,
        in_specs=[VMEM],
        out_specs=[VMEM, VMEM],
        out_shape=[jax.ShapeDtypeStruct((128, 512), F32), jax.ShapeDtypeStruct((4, 32, 128), F32)],
        scratch_shapes=[pltpu.VMEM((512, 128), F32), pltpu.VMEM((128, 128), F32)],
        compiler_params=PARAMS,
    )(c)


def rows_kernel(parts_ref, f1_ref, out_ref):
    row = jnp.sum(parts_ref[...], axis=0, keepdims=True)
    block = jnp.concatenate([row[:, i * 32 : (i + 1) * 32] for i in range(4)] * 2, 0)
    image = mm_exact(block, f1_ref[...], NN)
    image = jnp.concatenate([image[i : i + 1] for i in range(4)], 1)
    out_ref[...] = jnp.broadcast_to(image[None], out_ref.shape)


def image_rows(parts, f1):
    return pl.pallas_call(
        rows_kernel,
        in_specs=[VMEM, VMEM],
        out_specs=VMEM,
        out_shape=jax.ShapeDtypeStruct((128, 1, 256), F32),
        compiler_params=PARAMS,
    )(parts, f1)


def sum_kernel(parts_ref, out_ref):
    total = jnp.sum(parts_ref[...], axis=0)
    total = total + pltpu.roll(total, 4, 0)
    out_ref[...] = jnp.broadcast_to(total[None], out_ref.shape)


def sum_for_all(parts):
    total = pl.pallas_call(
        sum_kernel,
        in_specs=[VMEM],
        out_specs=VMEM,
        out_shape=jax.ShapeDtypeStruct((64, 8, 128), F32),
        compiler_params=PARAMS,
    )(parts.reshape(64, 8, 128))
    return total.reshape(128, 4, 128)


def inverse_factor(normal):
    rows, lanes = iota((64, 128), 0), iota((64, 128), 1)
    m = jnp.concatenate([normal, jnp.where(rows == lanes, 1.0, 0.0)[:, :64].astype(F32)], 1)
    blocks = [m[8 * k : 8 * k + 8] for k in range(8)]
    for k in range(8):
        row = [blocks[k][i : i + 1] for i in range(8)]
        pivot = {}
        for i in range(8):
            for l in range(i, 8):
                entry = blocks[k][i : i + 1, 8 * k + l : 8 * k + l + 1]
                pivot[i, l] = jnp.broadcast_to(entry, (1, 128))
        factor, taken = {}, []
        for i in range(8):
            inverse = 1.0 / pivot[i, i]
            taken.append(row[i] * inverse)
            for l in range(i + 1, 8):
                factor[i, l] = pivot[i, l] * inverse
            for l in range(i + 1, 8):
                row[l] = row[l] - pivot[i, l] * taken[i]
                for n in range(l, 8):
                    pivot[l, n] = pivot[l, n] - factor[i, l] * pivot[i, n]
        for i in reversed(range(8)):
            for l in range(i + 1, 8):
                taken[i] = taken[i] - factor[i, l] * taken[l]
        blocks[k] = jnp.concatenate(row, 0)
        for t in range(k + 1, 8):
            rest = blocks[t]
            for i in range(8):
                at = 8 * k + i
                rest = rest - jnp.broadcast_to(blocks[t][:, at : at + 1], (8, 128)) * taken[i]
            blocks[t] = rest
    m = jnp.concatenate(blocks, 0)
    diagonal = jnp.sum(jnp.where(rows == lanes, m, 0.0), axis=1, keepdims=True)
    return m[:, 64:] * lax.rsqrt(diagonal)


def second_kernel(gx_ref, parts_ref, e_ref, c_ref, new_ref, part_ref, i_ref, y_ref, c_vmem, sem):
    copy = pltpu.make_async_copy(c_ref.at[:, :, pl.ds(0, 128)], c_vmem, sem)
    copy.start()
    rows = jnp.sum(parts_ref[...].reshape(4, 32, 256), axis=0)
    for i in range(4):
        i_ref[pl.ds(i, 32, stride=4), :] = rows[:, i * 64 : (i + 1) * 64]
    image = i_ref[...]
    normal = mm_exact(image, image, TN)
    projected = split(mm_f32(image, e_ref[...], TN))
    inverse = inverse_factor(normal)
    basis = mm_exact(image, inverse, NT)
    i_ref[...] = basis * math.sqrt(128)
    new_ref[...] = i_ref[pl.ds(pl.multiple_of(32 * gx_ref[0], 32), 32), :]
    y = mm_f32(basis, mm3(split(inverse), projected, NN), NN)
    for r in range(4):
        y_ref[pl.ds(r, 128, stride=4), :] = y[:, r * 128 : (r + 1) * 128]
    yt = split(y_ref[...].T)
    both = jnp.concatenate(yt, 0)
    low = iota((64, 128), 1) < 64
    copy.wait()

    def two(i, _):
        c = [c_vmem[:, 2 * i + k].reshape(512, 128) for k in range(2)]
        ch, cl = split(jnp.concatenate(c, 1))
        o = mm(both, ch, NN)
        o = o[:128] + o[128:] + mm(yt[0], cl, NN)
        halves = [o[:64, at : at + 128] + pltpu.roll(o[64:, at : at + 128], 64, 1) for at in (0, 128)]
        part_ref[i] = jnp.where(low, halves[0], pltpu.roll(halves[1], 64, 1))
        return 0

    lax.fori_loop(0, 8, two, 0, unroll=True)


def second_image(gx, parts, e, c):
    return pl.pallas_call(
        second_kernel,
        in_specs=[SMEM, VMEM, VMEM, HBM],
        out_specs=[VMEM, VMEM],
        out_shape=[jax.ShapeDtypeStruct((32, 64), F32), jax.ShapeDtypeStruct((8, 64, 128), F32)],
        scratch_shapes=[
            pltpu.VMEM((128, 64), F32),
            pltpu.VMEM((512, 128), F32),
            pltpu.VMEM((4, 16, 128, 128), F32),
            pltpu.SemaphoreType.DMA,
        ],
        compiler_params=PARAMS,
    )(gx, parts, e, c)


def last_kernel(gy_ref, image_ref, new_ref):
    normal = jnp.zeros((64, 64), F32)
    for i in range(8):
        normal += mm_exact(image_ref[i], image_ref[i], NT)
    inverse = inverse_factor(normal)
    pair = image_ref[gy_ref[0] >> 1]
    mine = jnp.where(gy_ref[0] & 1 == 0, pair[:, :64], pair[:, 64:])
    new_ref[...] = mm_exact(mine.T, inverse, NT) * math.sqrt(1024)


def last_factor(gy, image):
    return pl.pallas_call(
        last_kernel,
        in_specs=[SMEM, VMEM],
        out_specs=VMEM,
        out_shape=jax.ShapeDtypeStruct((64, 64), F32),
        compiler_params=PARAMS,
    )(gy, image)


def to_all(x, names=ALL):
    return lax.all_to_all(x, names, 0, 0, tiled=True)


def in_hbm(x):
    return pltpu.with_memory_space_constraint(x, pltpu.HBM)


def swap(x):
    return lax.ppermute(x, "gz", [(0, 1), (1, 0)])


def per_device(tensor, factor_one, factor_two, factor_three, species_factor):
    gx, gy, gz = (lax.axis_index(name).astype(jnp.int32) for name in ALL)

    t = in_hbm(tensor.transpose(0, 1, 3, 2))
    factors = jnp.concatenate([factor_three, jnp.pad(species_factor.T, ((0, 48), (0, 32)))], 1)
    own_a, peer_a, ready = core_cut(0, gz[None], t, factors)
    own_b, peer_b = core_cut(1, gz[None], t, factors, ready)
    sent = merge_first(gx[None], own_a, swap(peer_a), factor_two)
    sent = merge_second(own_b, swap(peer_b), sent)
    c = to_all(sent, ("gx", "gy")).reshape(4, 16, 136, 128)

    e, gram = first_gram(c)
    rows = image_rows(to_all(gram.reshape(128, 1, 128)).reshape(128, 128), factor_one)
    new_one, second_part = second_image(gx[None], to_all(rows).reshape(128, 256), e, c)
    second = to_all(sum_for_all(to_all(second_part.reshape(128, 4, 128)))).reshape(8, 64, 128)
    new_two = last_factor(gy[None], second)
    return new_one, new_two


def solution(mesh):
    in_specs = (P("gx", "gy", "gz", None), P("gx", None), P("gy", None), P("gz", None), P())
    out_specs = (P("gx", None), P("gy", None))
    return jax.shard_map(
        per_device, mesh=mesh, in_specs=in_specs, out_specs=out_specs, check_vma=False
    )
```

```python
import functools
import math

import jax
import jax.numpy as jnp
from jax import lax
from jax.experimental import pallas as pl
from jax.experimental.pallas import tpu as pltpu
from jax.sharding import PartitionSpec as P

F32, BF16 = jnp.float32, jnp.bfloat16
NN = (((1,), (0,)), ((), ()))
NT = (((1,), (1,)), ((), ()))
TN = (((0,), (0,)), ((), ()))
ALL = ("gx", "gy", "gz")
PAIRS = (12, 4)
SLOTS = 6
VMEM = pl.BlockSpec(memory_space=pltpu.VMEM)
PARAMS = pltpu.CompilerParams(vmem_limit_bytes=12 << 20)
LARGE = pltpu.CompilerParams(vmem_limit_bytes=28 << 20)
HBM = pl.BlockSpec(memory_space=pltpu.HBM)
SMEM = pl.BlockSpec(memory_space=pltpu.SMEM)


def split(x):
    hi = x.astype(BF16)
    return hi, (x - hi.astype(F32)).astype(BF16)


def mm(a, b, dims):
    return lax.dot_general(a, b, dims, preferred_element_type=F32)


def mm3(a, b, dims):
    return mm(a[0], b[0], dims) + (mm(a[0], b[1], dims) + mm(a[1], b[0], dims))


def mm_f32(a, b, dims):
    return mm3(split(a), split(b), dims)


def mm_exact(a, b, dims):
    return lax.dot_general(a, b, dims, precision=lax.Precision.HIGHEST, preferred_element_type=F32)


def wide(w):
    zero = jnp.zeros_like(w[0])
    return jnp.concatenate([jnp.concatenate(w, 1), jnp.concatenate([w[0], zero], 1)], 0)


def mm_wide(x, w):
    y = mm(jnp.concatenate(split(x), 1), w, NN)
    return y[:, :128] + y[:, 128:]


def iota(shape, dim):
    return lax.broadcasted_iota(jnp.int32, shape, dim)


def ones_where(mask):
    return jnp.where(mask, 1.0, 0.0).astype(BF16)


def spread(left, x, right, mask):
    return tuple(
        jnp.where(mask, mm(mm(left, part, NN).astype(BF16), right, NN), 0.0).astype(BF16)
        for part in split(x)
    )


def core_kernel(chunk, gz_ref, t_hbm, factors_ref, *rest):
    first, pairs = (0, PAIRS[0]) if chunk == 0 else PAIRS
    if chunk == 0:
        own_out, peer_hbm, ready_ref, *scratch = rest
        own_ref = own_out
    else:
        ready_ref, own_out, peer_hbm, own_ref, *scratch = rest
    peer_ref, t_vmem, xa_ref, xb_ref, sems, out_sems, ready_sem = scratch
    skip = 2 * chunk

    def copy(i):
        slot = i % SLOTS
        return pltpu.make_async_copy(t_hbm.at[pl.ds(2 * (first + i), 2)], t_vmem.at[slot], sems.at[slot])

    def copy_ready():
        return pltpu.make_async_copy(t_hbm.at[pl.ds(2 * PAIRS[0], 4)], ready_ref, ready_sem)

    def copies_out(i):
        ends = [(peer_ref, peer_hbm)] + ([(own_ref, own_out)] if chunk == 1 else [])
        return [
            pltpu.make_async_copy(ref.at[:, :, pl.ds(i, 2)], hbm.at[:, :, pl.ds(i, 2)], out_sems.at[k, i // 2])
            for k, (ref, hbm) in enumerate(ends)
        ]

    for i in range(skip, min(SLOTS, pairs)):
        copy(i).start()

    q = ((iota((128, 16), 0) >> 3) + 8 * gz_ref[0]) & 15
    rows = ones_where(q == iota((128, 16), 1))
    columns = ones_where(iota((32, 256), 0) == (iota((32, 256), 1) & 31))
    same = (iota((128, 256), 0) & 7) == (iota((128, 256), 1) >> 5)
    sf = spread(rows, factors_ref[:16, 64:96], columns, same)
    rows = ones_where((iota((128, 64), 0) & 63) == iota((128, 64), 1))
    r = (iota((64, 128), 1) >> 3 << 2) + (iota((64, 128), 1) & 3)
    columns = ones_where(iota((64, 128), 0) == r)
    same = (iota((128, 128), 0) >> 6) == ((iota((128, 128), 1) >> 2) & 1)
    w3 = wide(spread(rows, factors_ref[:, :64], columns, same))

    def contract_s(t_ref, xs_ref):
        for g in range(8):
            at = slice(g * 8, g * 8 + 8)
            th, tl = split(jnp.concatenate([t_ref[a, at].reshape(256, 64) for a in range(2)], 1))
            y = mm(sf[0], jnp.concatenate([th, tl], 1), NN)
            x = y[:, :128] + y[:, 128:] + mm(sf[1], th, NN)
            xs_ref[:, at, :] = x.reshape(16, 8, 128)

    def contract_c(i, xs_ref):
        for k in range(8):
            o = mm_wide(xs_ref[2 * k : 2 * k + 2].reshape(128, 128), w3)
            o = o.T.reshape(16, 8, 128)
            if k < 4:
                own_ref[:, k, i] = o
            else:
                peer_ref[:, k - 4, i] = o

    def finish(i):
        contract_c(i, xa_ref)
        contract_c(i + 1, xb_ref)
        for out in copies_out(i):
            out.start()

    def two_pairs(step, _):
        i = 2 * step
        copy(i).wait()
        contract_s(t_vmem.at[i % SLOTS], xa_ref)
        copy(i + 1).wait()
        contract_s(t_vmem.at[(i + 1) % SLOTS], xb_ref)
        finish(i)

        @pl.when(i + SLOTS < pairs)
        def _():
            copy(i + SLOTS).start()
            copy(i + SLOTS + 1).start()

        if chunk == 0:

            @pl.when(i + SLOTS == pairs)
            def _():
                copy_ready().start()

        return 0

    if chunk == 1:
        contract_s(ready_ref.at[pl.ds(0, 2)], xa_ref)
        contract_s(ready_ref.at[pl.ds(2, 2)], xb_ref)
        finish(0)
    lax.fori_loop(chunk, pairs // 2, two_pairs, 0)
    for i in range(0, pairs, 2):
        for out in copies_out(i):
            out.wait()
    if chunk == 0:
        copy_ready().wait()


def core_cut(chunk, gz, tensor, factors, *ready):
    pairs = PAIRS[chunk]
    shape, fetched = (16, 4, pairs, 8, 128), (4, 64, 32, 64)
    peer = pltpu.HBM(shape, F32)
    if chunk == 0:
        out_specs, out_shape = [VMEM, HBM, VMEM], [pltpu.VMEM(shape, F32), peer, pltpu.VMEM(fetched, F32)]
    else:
        out_specs, out_shape = [HBM, HBM], [peer, peer]
    return pl.pallas_call(
        functools.partial(core_kernel, chunk),
        in_specs=[SMEM, HBM, VMEM] + [VMEM] * chunk,
        out_specs=out_specs,
        out_shape=out_shape,
        scratch_shapes=[pltpu.VMEM(shape, F32)] * (1 + chunk)
        + [
            pltpu.VMEM((SLOTS, 2, 64, 32, 64), F32),
            pltpu.VMEM((16, 64, 128), F32),
            pltpu.VMEM((16, 64, 128), F32),
            pltpu.SemaphoreType.DMA((SLOTS,)),
            pltpu.SemaphoreType.DMA((2, pairs // 2)),
            pltpu.SemaphoreType.DMA,
        ],
        compiler_params=LARGE,
    )(gz, tensor, factors, *ready)


def merge_first_kernel(gx_ref, own_ref, other_hbm, f2_ref, out_ref, other_ref, sems):
    rows = 8 * PAIRS[0]
    copies = [
        pltpu.make_async_copy(other_hbm.at[pl.ds(2 * g, 2)], other_ref.at[pl.ds(2 * g, 2)], sems.at[g])
        for g in range(8)
    ]
    for copy in copies:
        copy.start()
    f2 = f2_ref[pl.ds(pl.multiple_of(16 * gx_ref[0], 16), 16), :]
    f2 = jnp.concatenate([f2[:8], f2[8:]], 1)
    out_ref[:, 128:] = jnp.broadcast_to(f2[None], (64, 8, 128))
    for g in range(16):
        if g % 2 == 0:
            copies[g // 2].wait()
        out_ref[4 * g : 4 * g + 4, :rows] = (own_ref[g] + other_ref[g]).reshape(4, rows, 128)


def merge_second_kernel(own_ref, other_hbm, sent_ref, out_ref, other_ref, sems):
    rows = 8 * PAIRS[1]
    copies = [
        pltpu.make_async_copy(other_hbm.at[pl.ds(4 * g, 4)], other_ref.at[pl.ds(4 * g, 4)], sems.at[g])
        for g in range(4)
    ]
    for copy in copies:
        copy.start()
    for g in range(16):
        if g % 4 == 0:
            copies[g // 4].wait()
        total = (own_ref[g] + other_ref[g]).reshape(4, rows, 128)
        out_ref[4 * g : 4 * g + 4, 8 * PAIRS[0] : 128] = total


def merge_first(gx, own, other, f2):
    return pl.pallas_call(
        merge_first_kernel,
        in_specs=[SMEM, VMEM, HBM, VMEM],
        out_specs=VMEM,
        out_shape=pltpu.VMEM((64, 136, 128), F32),
        scratch_shapes=[pltpu.VMEM(own.shape, F32), pltpu.SemaphoreType.DMA((8,))],
        compiler_params=PARAMS,
    )(gx, own, in_hbm(other), f2)


def merge_second(own, other, sent):
    return pl.pallas_call(
        merge_second_kernel,
        in_specs=[VMEM, HBM, VMEM],
        out_specs=VMEM,
        out_shape=pltpu.VMEM((64, 136, 128), F32),
        scratch_shapes=[pltpu.VMEM(other.shape, F32), pltpu.SemaphoreType.DMA((4,))],
        input_output_aliases={2: 0},
        compiler_params=PARAMS,
    )(own, in_hbm(other), sent)


def first_kernel(c_ref, e_ref, gram_ref, fp_ref, g_ref):
    low = iota((8, 128), 1) < 64
    total = jnp.zeros((512, 256), F32)
    for y in range(16):
        top, bottom = [], []
        for x in range(4):
            f2 = c_ref[x, y, 128:]
            turned = pltpu.roll(f2, 64, 1)
            top += [jnp.where(low, f2, 0.0), jnp.where(low, turned, 0.0)]
            bottom += [jnp.where(low, 0.0, turned), jnp.where(low, 0.0, f2)]
        w = wide(split(jnp.concatenate(top + bottom, 0)))
        total += mm(jnp.concatenate(split(c_ref[:, y, :128].reshape(512, 128)), 1), w, NN)
    fp_ref[...] = total[:, :128] + total[:, 128:]
    gram, cross = jnp.zeros((128, 128), F32), jnp.zeros((128, 128), F32)
    for r in range(4):
        e = fp_ref[pl.ds(r, 128, stride=4), :]
        e_ref[:, r * 128 : (r + 1) * 128] = e
        eh, el = split(e)
        gram += mm(eh, eh, NT) + mm(el, el, NT)
        cross += mm(eh, el, NT)
    g_ref[...] = gram + (cross + cross.T)
    group = iota((32, 128), 1) >> 5
    rows = [g_ref[pl.ds(i, 32, stride=4), :] for i in range(4)]
    for x in range(4):
        block = jnp.zeros((32, 128), F32)
        for i in range(4):
            moved = pltpu.roll(rows[i], 32 * ((i - x) % 4), 1) if i != x else rows[i]
            block = jnp.where(group == i, moved, block)
        gram_ref[x] = block


def first_gram(c):
    return pl.pallas_call(
        first_kernel,
        in_specs=[VMEM],
        out_specs=[VMEM, VMEM],
        out_shape=[jax.ShapeDtypeStruct((128, 512), F32), jax.ShapeDtypeStruct((4, 32, 128), F32)],
        scratch_shapes=[pltpu.VMEM((512, 128), F32), pltpu.VMEM((128, 128), F32)],
        compiler_params=PARAMS,
    )(c)


def rows_kernel(parts_ref, f1_ref, out_ref):
    row = jnp.sum(parts_ref[...], axis=0, keepdims=True)
    block = jnp.concatenate([row[:, i * 32 : (i + 1) * 32] for i in range(4)] * 2, 0)
    image = mm_exact(block, f1_ref[...], NN)
    image = jnp.concatenate([image[i : i + 1] for i in range(4)], 1)
    out_ref[...] = jnp.broadcast_to(image[None], out_ref.shape)


def image_rows(parts, f1):
    return pl.pallas_call(
        rows_kernel,
        in_specs=[VMEM, VMEM],
        out_specs=VMEM,
        out_shape=jax.ShapeDtypeStruct((128, 1, 256), F32),
        compiler_params=PARAMS,
    )(parts, f1)


def sum_kernel(parts_ref, out_ref):
    total = jnp.sum(parts_ref[...], axis=0)
    total = total + pltpu.roll(total, 4, 0)
    out_ref[...] = jnp.broadcast_to(total[None], out_ref.shape)


def sum_for_all(parts):
    total = pl.pallas_call(
        sum_kernel,
        in_specs=[VMEM],
        out_specs=VMEM,
        out_shape=jax.ShapeDtypeStruct((64, 8, 128), F32),
        compiler_params=PARAMS,
    )(parts.reshape(64, 8, 128))
    return total.reshape(128, 4, 128)


def inverse_factor(normal):
    rows, lanes = iota((64, 128), 0), iota((64, 128), 1)
    m = jnp.concatenate([normal, jnp.where(rows == lanes, 1.0, 0.0)[:, :64].astype(F32)], 1)
    blocks = [m[8 * k : 8 * k + 8] for k in range(8)]
    for k in range(8):
        row = [blocks[k][i : i + 1] for i in range(8)]
        pivot = {}
        for i in range(8):
            for l in range(i, 8):
                entry = blocks[k][i : i + 1, 8 * k + l : 8 * k + l + 1]
                pivot[i, l] = jnp.broadcast_to(entry, (1, 128))
        factor, taken = {}, []
        for i in range(8):
            inverse = 1.0 / pivot[i, i]
            taken.append(row[i] * inverse)
            for l in range(i + 1, 8):
                factor[i, l] = pivot[i, l] * inverse
            for l in range(i + 1, 8):
                row[l] = row[l] - pivot[i, l] * taken[i]
                for n in range(l, 8):
                    pivot[l, n] = pivot[l, n] - factor[i, l] * pivot[i, n]
        for i in reversed(range(8)):
            for l in range(i + 1, 8):
                taken[i] = taken[i] - factor[i, l] * taken[l]
        blocks[k] = jnp.concatenate(row, 0)
        for t in range(k + 1, 8):
            rest = blocks[t]
            for i in range(8):
                at = 8 * k + i
                rest = rest - jnp.broadcast_to(blocks[t][:, at : at + 1], (8, 128)) * taken[i]
            blocks[t] = rest
    m = jnp.concatenate(blocks, 0)
    diagonal = jnp.sum(jnp.where(rows == lanes, m, 0.0), axis=1, keepdims=True)
    return m[:, 64:] * lax.rsqrt(diagonal)


def second_kernel(gx_ref, parts_ref, e_ref, c_ref, new_ref, part_ref, i_ref, y_ref, c_vmem, sem):
    copy = pltpu.make_async_copy(c_ref.at[:, :, pl.ds(0, 128)], c_vmem, sem)
    copy.start()
    rows = jnp.sum(parts_ref[...].reshape(4, 32, 256), axis=0)
    for i in range(4):
        i_ref[pl.ds(i, 32, stride=4), :] = rows[:, i * 64 : (i + 1) * 64]
    image = i_ref[...]
    normal = mm_exact(image, image, TN)
    projected = split(mm_f32(image, e_ref[...], TN))
    inverse = inverse_factor(normal)
    basis = mm_exact(image, inverse, NT)
    i_ref[...] = basis * math.sqrt(128)
    new_ref[...] = i_ref[pl.ds(pl.multiple_of(32 * gx_ref[0], 32), 32), :]
    y = mm_f32(basis, mm3(split(inverse), projected, NN), NN)
    for r in range(4):
        y_ref[pl.ds(r, 128, stride=4), :] = y[:, r * 128 : (r + 1) * 128]
    yt = split(y_ref[...].T)
    both = jnp.concatenate(yt, 0)
    low = iota((64, 128), 1) < 64
    copy.wait()

    def two(i, _):
        c = [c_vmem[:, 2 * i + k].reshape(512, 128) for k in range(2)]
        ch, cl = split(jnp.concatenate(c, 1))
        o = mm(both, ch, NN)
        o = o[:128] + o[128:] + mm(yt[0], cl, NN)
        halves = [o[:64, at : at + 128] + pltpu.roll(o[64:, at : at + 128], 64, 1) for at in (0, 128)]
        part_ref[i] = jnp.where(low, halves[0], pltpu.roll(halves[1], 64, 1))
        return 0

    lax.fori_loop(0, 8, two, 0, unroll=True)


def second_image(gx, parts, e, c):
    return pl.pallas_call(
        second_kernel,
        in_specs=[SMEM, VMEM, VMEM, HBM],
        out_specs=[VMEM, VMEM],
        out_shape=[jax.ShapeDtypeStruct((32, 64), F32), jax.ShapeDtypeStruct((8, 64, 128), F32)],
        scratch_shapes=[
            pltpu.VMEM((128, 64), F32),
            pltpu.VMEM((512, 128), F32),
            pltpu.VMEM((4, 16, 128, 128), F32),
            pltpu.SemaphoreType.DMA,
        ],
        compiler_params=PARAMS,
    )(gx, parts, e, c)


def last_kernel(gy_ref, image_ref, new_ref):
    normal = jnp.zeros((64, 64), F32)
    for i in range(8):
        normal += mm_exact(image_ref[i], image_ref[i], NT)
    inverse = inverse_factor(normal)
    pair = image_ref[gy_ref[0] >> 1]
    mine = jnp.where(gy_ref[0] & 1 == 0, pair[:, :64], pair[:, 64:])
    new_ref[...] = mm_exact(mine.T, inverse, NT) * math.sqrt(1024)


def last_factor(gy, image):
    return pl.pallas_call(
        last_kernel,
        in_specs=[SMEM, VMEM],
        out_specs=VMEM,
        out_shape=jax.ShapeDtypeStruct((64, 64), F32),
        compiler_params=PARAMS,
    )(gy, image)


def to_all(x, names=ALL):
    return lax.all_to_all(x, names, 0, 0, tiled=True)


def in_hbm(x):
    return pltpu.with_memory_space_constraint(x, pltpu.HBM)


def swap(x):
    return lax.ppermute(x, "gz", [(0, 1), (1, 0)])


def per_device(tensor, factor_one, factor_two, factor_three, species_factor):
    gx, gy, gz = (lax.axis_index(name).astype(jnp.int32) for name in ALL)

    t = in_hbm(tensor.transpose(0, 1, 3, 2))
    factors = jnp.concatenate([factor_three, jnp.pad(species_factor.T, ((0, 48), (0, 32)))], 1)
    own_a, peer_a, ready = core_cut(0, gz[None], t, factors)
    own_b, peer_b = core_cut(1, gz[None], t, factors, ready)
    sent = merge_first(gx[None], own_a, swap(peer_a), factor_two)
    sent = merge_second(own_b, swap(peer_b), sent)
    c = to_all(sent, ("gx", "gy")).reshape(4, 16, 136, 128)

    e, gram = first_gram(c)
    rows = image_rows(to_all(gram.reshape(128, 1, 128)).reshape(128, 128), factor_one)
    new_one, second_part = second_image(gx[None], to_all(rows).reshape(128, 256), e, c)
    second = to_all(sum_for_all(to_all(second_part.reshape(128, 4, 128)))).reshape(8, 64, 128)
    new_two = last_factor(gy[None], second)
    return new_one, new_two


def solution(mesh):
    in_specs = (P("gx", "gy", "gz", None), P("gx", None), P("gy", None), P("gz", None), P())
    out_specs = (P("gx", None), P("gy", None))
    return jax.shard_map(
        per_device, mesh=mesh, in_specs=in_specs, out_specs=out_specs, check_vma=False
    )
```
